32 devices in a mesh: dp: 16 (over z, y, core), tensor: 2 (over x).
Axes of the slice: x: 2, y: 2, z: 4, core: 2. Of those that a mesh axis runs over, the one named last changes fastest.
Arguments:
- tokens: bfloat16 [6144, 2048], P(('dp', 'tensor')), may hold values from -6 to 6
- segment_ids: int32 [16, 384], P('dp'), may hold values from 0 to 3, as said below
- cotangent: bfloat16 [6144, 2048], P(('dp', 'tensor')), may hold values from -6 to 6
- w_qkv: float32 [3, 2048, 2048], P(None, 'dp', 'tensor'), may hold values from -0.125 to 0.125
- m_qkv: float32 [3, 2048, 2048], P(None, 'dp', 'tensor'), may hold values from -51.733223 to 51.733223
- v_qkv: float32 [3, 2048, 2048], P(None, 'dp', 'tensor'), may hold values from 307.2 to 1228.8
- w_out: float32 [2048, 2048], P('tensor', 'dp'), may hold values from -0.5 to 0.5
- m_out: float32 [2048, 2048], P('tensor', 'dp'), may hold values from -14.109061 to 14.109061
- v_out: float32 [2048, 2048], P('tensor', 'dp'), may hold values from 18.432 to 76.8
- w_gate_up: float32 [2, 2048, 5632], P(None, 'dp', 'tensor'), may hold values from -0.125 to 0.125
- m_gate_up: float32 [2, 2048, 5632], P(None, 'dp', 'tensor'), may hold values from -15.676734 to 15.676734
- v_gate_up: float32 [2, 2048, 5632], P(None, 'dp', 'tensor'), may hold values from 27.648 to 110.592
- w_down: float32 [5632, 2048], P('tensor', 'dp'), may hold values from -0.078125 to 0.078125
- m_down: float32 [5632, 2048], P('tensor', 'dp'), may hold values from -31.353468 to 31.353468
- v_down: float32 [5632, 2048], P('tensor', 'dp'), may hold values from 110.592 to 442.368
- b_qkv: float32 [3, 2048], P(None, 'tensor'), may hold values from -3 to 3
- m_bias: float32 [3, 2048], P(None, 'tensor'), may hold values from -42.327183 to 42.327183
- v_bias: float32 [3, 2048], P(None, 'tensor'), may hold values from 196.608 to 786.432
- ln_params: float32 [4, 2048], replicated, may hold values from -0.3 to 1.3, as said below
- m_norm: float32 [4, 2048], replicated, may hold values from -51.733223 to 51.733223
- v_norm: float32 [4, 2048], replicated, may hold values from 307.2 to 1228.8
Outputs:
- output: bfloat16 [6144, 2048], P(('dp', 'tensor'))
- input_grad: float32 [6144, 2048], P(('dp', 'tensor'))
- m_qkv_new: float32 [3, 2048, 2048], P(None, 'dp', 'tensor')
- v_qkv_new: float32 [3, 2048, 2048], P(None, 'dp', 'tensor')
- w_qkv_new: float32 [3, 2048, 2048], P(None, 'dp', 'tensor')
- m_out_new: float32 [2048, 2048], P('tensor', 'dp')
- v_out_new: float32 [2048, 2048], P('tensor', 'dp')
- w_out_new: float32 [2048, 2048], P('tensor', 'dp')
- m_gate_up_new: float32 [2, 2048, 5632], P(None, 'dp', 'tensor')
- v_gate_up_new: float32 [2, 2048, 5632], P(None, 'dp', 'tensor')
- w_gate_up_new: float32 [2, 2048, 5632], P(None, 'dp', 'tensor')
- m_down_new: float32 [5632, 2048], P('tensor', 'dp')
- v_down_new: float32 [5632, 2048], P('tensor', 'dp')
- w_down_new: float32 [5632, 2048], P('tensor', 'dp')
- m_bias_new: float32 [3, 2048], P(None, 'tensor')
- v_bias_new: float32 [3, 2048], P(None, 'tensor')
- b_qkv_new: float32 [3, 2048], P(None, 'tensor')
- m_norm_new: float32 [4, 2048], replicated
- v_norm_new: float32 [4, 2048], replicated
- ln_params_new: float32 [4, 2048], replicated
The draws below stay inside these ranges and needn't reach their ends.
Inputs may be any that keep to these rules, and one draw needn't show every extreme that they name: `segment_ids`: each row is one sequence; its numbers never fall along the row, and a document is a run of equal numbers. No document begins at a place from 144 to 239. `ln_params`: rows 0 and 2 are gains, rows 1 and 3 biases.
All inputs are finite; a program needn't handle non-finite values.
Results may differ from the reference program's by a relative error of at most 0.013.
Values may be sent and summed in bfloat16 or wider, within the bound.
No kernel may reach another device: no remote copies, remote signals or barrier semaphores. Data moves between devices by JAX's collectives and lax.ppermute only.
A program may use at most 320 MiB of HBM per device.

```python
import math
import jax
import jax.numpy as jnp
from jax import lax

D = 2048
HEADS = 32
HD = 64
ROT = 16
FF = 5632
LEN = 384
STEP_COUNT = 10
SEQS = 16
TOKENS = 6144


def draw_segment_ids(key, part):
    key = jax.random.fold_in(key, 11)
    quarter = LEN // 4
    lower_end = LEN * 3 // 8
    picks = jax.random.randint(key, (SEQS, 3), 0, LEN - 1 - quarter)
    cuts = picks + 1
    cuts = jnp.where(cuts < lower_end, cuts, cuts + quarter)
    positions = jnp.arange(LEN, dtype=jnp.int32)
    return jnp.sum((positions[None, :, None] >= cuts[:, None, :]).astype(jnp.int32), axis=2)


def draw_ln_params(key, part):
    key = jax.random.fold_in(key, 23)
    spread = jax.random.uniform(key, (4, D), jnp.float32, -0.5, 0.5)
    parity = jnp.arange(4, dtype=jnp.int32)[:, None] % 2
    return jnp.where(parity == 0, 1.0 + 0.6 * spread, 0.6 * spread)


def levels(key, dims, cuts, low, largest):
    loudness = 1.0
    for dim, parts in cuts:
        heights = jax.random.uniform(jax.random.fold_in(jax.random.fold_in(key, 6), dim), (parts,), jnp.float32, low / len(cuts), largest / len(cuts))
        loudness = loudness * jnp.repeat(jnp.exp(heights), dims[dim] // parts).reshape((-1,) + (1,) * (len(dims) - 1 - dim))
    return loudness


def normal_values(stream_key, shape, width, limit, cuts=(), kind=jnp.bfloat16):
    entries = width * jax.random.normal(stream_key, shape, jnp.float32)
    if cuts:
        entries = entries * levels(stream_key, shape, cuts, -0.22, 0.18)
    return jnp.clip(entries, -limit, limit).astype(kind)


def setup_inputs(seed: int = 0) -> dict:
    key_list = jax.random.split(jax.random.key(seed), 22)
    tokens = normal_values(key_list[0], (TOKENS, D), 1.0, 6.0, ((0, 32),))
    segment_ids = draw_segment_ids(jax.random.fold_in(key_list[21], 71), 0)
    cotangent = normal_values(key_list[2], (TOKENS, D), 1.0, 6.0, ((0, 32),))
    w_qkv = normal_values(key_list[3], (3, D, D), D ** -0.5, 0.125, ((1, 16), (2, 2)), jnp.float32)
    m_qkv = normal_values(key_list[4], (3, D, D), (0.11 * TOKENS ** 0.5), 51.733223, ((1, 16), (2, 2)), jnp.float32)
    v_qkv = jnp.clip(jnp.exp(math.log(1228.8) - 1.3862944 * jax.random.uniform(key_list[5], (3, D, D), jnp.float32) ** levels(key_list[5], (3, D, D), ((1, 16), (2, 2)), -0.2, 0.2)), 307.2, 1228.8)
    w_out = normal_values(key_list[6], (D, D), (D // 16) ** -0.5, 0.5, ((0, 2), (1, 16)), jnp.float32)
    m_out = normal_values(key_list[7], (D, D), (0.03 * TOKENS ** 0.5), 14.109061, ((0, 2), (1, 16)), jnp.float32)
    v_out = jnp.clip(jnp.exp(math.log(76.8) - 1.4271164 * jax.random.uniform(key_list[8], (D, D), jnp.float32) ** levels(key_list[8], (D, D), ((0, 2), (1, 16)), -0.2, 0.2)), 18.432, 76.8)
    w_gate_up = normal_values(key_list[9], (2, D, FF), D ** -0.5, 0.125, ((1, 16), (2, 2)), jnp.float32)
    m_gate_up = normal_values(key_list[10], (2, D, FF), (0.033 * TOKENS ** 0.5), 15.676734, ((1, 16), (2, 2)), jnp.float32)
    v_gate_up = jnp.clip(jnp.exp(math.log(110.592) - 1.3862944 * jax.random.uniform(key_list[11], (2, D, FF), jnp.float32) ** levels(key_list[11], (2, D, FF), ((1, 16), (2, 2)), -0.2, 0.2)), 27.648, 110.592)
    w_down = normal_values(key_list[12], (FF, D), FF ** -0.5, 0.078125, ((0, 2), (1, 16)), jnp.float32)
    m_down = normal_values(key_list[13], (FF, D), (0.066 * TOKENS ** 0.5), 31.353468, ((0, 2), (1, 16)), jnp.float32)
    v_down = jnp.clip(jnp.exp(math.log(442.368) - 1.3862944 * jax.random.uniform(key_list[14], (FF, D), jnp.float32) ** levels(key_list[14], (FF, D), ((0, 2), (1, 16)), -0.2, 0.2)), 110.592, 442.368)
    b_qkv = normal_values(key_list[15], (3, D), 0.5, 3.0, ((1, 2),), jnp.float32)
    m_bias = normal_values(key_list[16], (3, D), (0.09 * TOKENS ** 0.5), 42.327183, ((1, 2),), jnp.float32)
    v_bias = jnp.clip(jnp.exp(math.log(786.432) - 1.3862944 * jax.random.uniform(key_list[17], (3, D), jnp.float32) ** levels(key_list[17], (3, D), ((1, 2),), -0.2, 0.2)), 196.608, 786.432)
    ln_params = draw_ln_params(jax.random.fold_in(key_list[21], 71), 0)
    m_norm = normal_values(key_list[19], (4, D), (0.11 * TOKENS ** 0.5), 51.733223, (), jnp.float32)
    v_norm = jnp.clip(jnp.exp(jax.random.uniform(key_list[20], (4, D), jnp.float32, math.log(307.2), math.log(1228.8))), 307.2, 1228.8)
    return dict(tokens=tokens, segment_ids=segment_ids, cotangent=cotangent, w_qkv=w_qkv, m_qkv=m_qkv, v_qkv=v_qkv, w_out=w_out, m_out=m_out, v_out=v_out, w_gate_up=w_gate_up, m_gate_up=m_gate_up, v_gate_up=v_gate_up, w_down=w_down, m_down=m_down, v_down=v_down, b_qkv=b_qkv, m_bias=m_bias, v_bias=v_bias, ln_params=ln_params, m_norm=m_norm, v_norm=v_norm)


EPS = 1e-05
NEG_FILL = -1000000000.0
BETA_ONE = 0.9
BETA_TWO = 0.95
ADAM_EPS = 1e-08
RATE_MATRIX = 0.01
RATE_OUT = 0.05
RATE_SMALL = 0.25
DECAY_MATRIX = 0.1
PRECISE = lax.Precision.HIGHEST

@jax.custom_vjp
def low(v):
    return lax.optimization_barrier(v.astype(jnp.bfloat16)).astype(jnp.float32)

@jax.custom_vjp
def low_back(v):
    return v

def low_keep(v):
    return (low(v), None)

def low_pass(kept, grad):
    return (grad,)

def back_keep(v):
    return (v, None)

def back_low(kept, grad):
    return (low(grad),)
low.defvjp(low_keep, low_pass)
low_back.defvjp(back_keep, back_low)

def norm_rows(row_data, gain_vec, shift_vec):
    average = lax.optimization_barrier(jnp.mean(row_data, axis=-1, keepdims=True))
    centered = row_data - average
    variance = lax.optimization_barrier(jnp.mean(centered * centered, axis=-1, keepdims=True))
    return centered * lax.rsqrt(variance + EPS) * gain_vec + shift_vec

def rotate(head_data, cos_part, sin_part):
    half_rot = cos_part.shape[-1]
    leading = head_data[..., :half_rot]
    trailing = head_data[..., half_rot:2 * half_rot]
    remains = head_data[..., 2 * half_rot:]
    return jnp.concatenate([leading * cos_part - trailing * sin_part, trailing * cos_part + leading * sin_part, remains], axis=-1)

def angles(length):
    positions = jnp.arange(length, dtype=jnp.int32).astype(jnp.float32)
    half_rot = ROT // 2
    frequency = 10000.0 ** (-2.0 * jnp.arange(half_rot, dtype=jnp.int32).astype(jnp.float32) / ROT)
    angle_table = positions[:, None] * frequency[None, :]
    return (jnp.cos(angle_table)[:, None, :], jnp.sin(angle_table)[:, None, :])

def adamw_update(weight, first_mom, second, gradient, step_rate, decay_rate):
    first_mom = BETA_ONE * first_mom + (1.0 - BETA_ONE) * gradient
    second = BETA_TWO * second + (1.0 - BETA_TWO) * gradient * gradient
    fix_first = 1.0 - BETA_ONE ** STEP_COUNT
    fix_second = 1.0 - BETA_TWO ** STEP_COUNT
    update = first_mom / fix_first / (jnp.sqrt(second / fix_second) + ADAM_EPS)
    return (first_mom, second, weight - step_rate * (update + decay_rate * weight))

def layer_step(row_data, doc_ids, w_qkv, b_qkv, w_out, w_gate_up, w_down, ln_params):
    length = row_data.shape[0]
    cos_part, sin_part = angles(length)
    positions = jnp.arange(length, dtype=jnp.int32)
    allowed = (positions[None, :] <= positions[:, None]) & (doc_ids[None, :] == doc_ids[:, None])
    score_scale = HD ** (-0.5)
    normed_a = low(norm_rows(row_data, ln_params[0], ln_params[1]))
    projected = jnp.einsum('td,kde->kte', normed_a, low(w_qkv), precision=PRECISE) + b_qkv[:, None, :]
    projected = low_back(projected)
    split_heads = projected.reshape(3, length, HEADS, HD)
    queries = low(rotate(split_heads[0], cos_part, sin_part))
    key_rows = low(rotate(split_heads[1], cos_part, sin_part))
    values = low(split_heads[2])
    scores = low_back(jnp.einsum('qhd,khd->hqk', queries, key_rows, precision=PRECISE) * score_scale)
    masked = jnp.where(allowed[None], scores, NEG_FILL)
    peak_score = lax.optimization_barrier(jnp.max(masked, axis=-1, keepdims=True))
    exponent = jnp.exp(masked - peak_score)
    probs = low(exponent / lax.optimization_barrier(jnp.sum(exponent, axis=-1, keepdims=True)))
    mixture = jnp.einsum('hqk,khd->qhd', probs, values, precision=PRECISE).reshape(length, HEADS * HD)
    mixture = low(low_back(mixture))
    branch = low_back(jnp.dot(mixture, low(w_out), precision=PRECISE))
    middle = row_data + branch
    normed_c = low(norm_rows(middle, ln_params[2], ln_params[3]))
    gate_up = low_back(jnp.einsum('td,kdf->ktf', normed_c, low(w_gate_up), precision=PRECISE))
    hidden = low(jax.nn.silu(gate_up[0]) * gate_up[1])
    result = low_back(jnp.dot(hidden, low(w_down), precision=PRECISE))
    return middle + result

def reference(tokens, segment_ids, cotangent, w_qkv, m_qkv, v_qkv, w_out, m_out, v_out, w_gate_up, m_gate_up, v_gate_up, w_down, m_down, v_down, b_qkv, m_bias, v_bias, ln_params, m_norm, v_norm):
    inputs_f = tokens.astype(jnp.float32).reshape(SEQS, LEN, D)
    back_rows = cotangent.astype(jnp.float32).reshape(SEQS, LEN, D)
    params = (w_qkv, b_qkv, w_out, w_gate_up, w_down, ln_params)

    def per_sequence(carry_sum, item):
        seq_rows, seq_ids, seq_back = item

        def closed(row_data, weight_qkv, bias_qkv, weight_out, weight_gate_up, weight_down, norm_params):
            return layer_step(row_data, seq_ids, weight_qkv, bias_qkv, weight_out, weight_gate_up, weight_down, norm_params)
        block_out, pull_back = jax.vjp(closed, seq_rows, w_qkv, b_qkv, w_out, w_gate_up, w_down, ln_params)
        gradients = pull_back(seq_back)
        carry_sum = jax.tree.map(jnp.add, carry_sum, tuple(gradients[1:]))
        return (carry_sum, (block_out, gradients[0]))
    zero_sums = jax.tree.map(jnp.zeros_like, params)
    grad_sums, (block_outs, input_grads) = lax.scan(per_sequence, zero_sums, (inputs_f, segment_ids, back_rows))
    m_qkv_new, v_qkv_new, w_qkv_new = adamw_update(w_qkv, m_qkv, v_qkv, grad_sums[0], RATE_MATRIX, DECAY_MATRIX)
    m_out_new, v_out_new, w_out_new = adamw_update(w_out, m_out, v_out, grad_sums[2], RATE_OUT, DECAY_MATRIX)
    m_gate_up_new, v_gate_up_new, w_gate_up_new = adamw_update(w_gate_up, m_gate_up, v_gate_up, grad_sums[3], RATE_MATRIX, DECAY_MATRIX)
    m_down_new, v_down_new, w_down_new = adamw_update(w_down, m_down, v_down, grad_sums[4], RATE_MATRIX, DECAY_MATRIX)
    m_bias_new, v_bias_new, b_qkv_new = adamw_update(b_qkv, m_bias, v_bias, grad_sums[1], RATE_SMALL, 0.0)
    m_norm_new, v_norm_new, ln_params_new = adamw_update(ln_params, m_norm, v_norm, grad_sums[5], RATE_SMALL, 0.0)
    output = block_outs.reshape(TOKENS, D).astype(jnp.bfloat16)
    input_grad = input_grads.reshape(TOKENS, D)
    return (output, input_grad, m_qkv_new, v_qkv_new, w_qkv_new, m_out_new, v_out_new, w_out_new, m_gate_up_new, v_gate_up_new, w_gate_up_new, m_down_new, v_down_new, w_down_new, m_bias_new, v_bias_new, b_qkv_new, m_norm_new, v_norm_new, ln_params_new)
```

```python
import jax
import jax.numpy as jnp
from jax import lax
from jax.sharding import Mesh
from jax.sharding import PartitionSpec as P

HD = 64
ROT = 16
STEP_COUNT = 10

EPS = 1e-05
NEG_FILL = -1000000000.0
BETA_ONE = 0.9
BETA_TWO = 0.95
ADAM_EPS = 1e-08
RATE_MATRIX = 0.01
RATE_OUT = 0.05
RATE_SMALL = 0.25
DECAY_MATRIX = 0.1

LOW = jnp.bfloat16
F32 = jnp.float32


def dot(left, right, left_dim, right_dim):
    return lax.dot_general(
        left, right, (((left_dim,), (right_dim,)), ((), ())), preferred_element_type=F32
    )


def swap(block, axis):
    return lax.ppermute(block, axis, [(0, 1), (1, 0)])


def pick(block, index, dim):
    return lax.dynamic_index_in_dim(block, index, dim, keepdims=False)


def in_order(own, other, index):
    first = index == 0
    return jnp.stack([jnp.where(first, own, other), jnp.where(first, other, own)])


def norm_stats(row_data):
    average = jnp.mean(row_data, axis=-1, keepdims=True)
    centered = row_data - average
    variance = jnp.mean(centered * centered, axis=-1, keepdims=True)
    scale = lax.rsqrt(variance + EPS)
    return centered * scale, scale


def norm_back(hat, scale, gain_vec, grad):
    scaled = grad * gain_vec
    row_grad = (
        scaled
        - jnp.mean(scaled, axis=-1, keepdims=True)
        - hat * jnp.mean(scaled * hat, axis=-1, keepdims=True)
    ) * scale
    return row_grad, jnp.sum(grad * hat, axis=0), jnp.sum(grad, axis=0)


def rotate(head_data, cos_part, sin_part):
    half_rot = cos_part.shape[-1]
    leading = head_data[..., :half_rot]
    trailing = head_data[..., half_rot : 2 * half_rot]
    remains = head_data[..., 2 * half_rot :]
    return jnp.concatenate(
        [
            leading * cos_part - trailing * sin_part,
            trailing * cos_part + leading * sin_part,
            remains,
        ],
        axis=-1,
    )


def angles(positions):
    half_rot = ROT // 2
    frequency = 10000.0 ** (-2.0 * jnp.arange(half_rot, dtype=jnp.int32).astype(F32) / ROT)
    angle_table = positions.astype(F32)[:, None] * frequency[None, :]
    return (jnp.cos(angle_table)[:, None, :], jnp.sin(angle_table)[:, None, :])


def adamw_update(weight, first_mom, second, gradient, step_rate, decay_rate):
    first_mom = BETA_ONE * first_mom + (1.0 - BETA_ONE) * gradient
    second = BETA_TWO * second + (1.0 - BETA_TWO) * gradient * gradient
    fix_first = 1.0 - BETA_ONE**STEP_COUNT
    fix_second = 1.0 - BETA_TWO**STEP_COUNT
    update = first_mom / fix_first / (jnp.sqrt(second / fix_second) + ADAM_EPS)
    return (first_mom, second, weight - step_rate * (update + decay_rate * weight))


def gather_rows(rows):
    half = rows.shape[1] // 2
    left, right = rows[:, :half], rows[:, half:]
    left_x = swap(left, "tensor")
    right_y = swap(right, "y")
    left_pair = jnp.stack([left, left_x])
    right_pair = jnp.stack([right, right_y])
    left_far = swap(left_pair, "y")
    right_far = swap(right_pair, "tensor")
    quad = jnp.concatenate(
        [jnp.stack([left_pair, left_far]), jnp.stack([right_pair, right_far], axis=1)], axis=-1
    )
    other = swap(quad, "core")
    return jnp.stack([quad, other]).reshape(-1, rows.shape[1])


def reduce_rows(left_side, right_side, right_dim):
    count = left_side.shape[0] // 2
    away = dot(left_side[count:], right_side, 1, right_dim).astype(LOW)
    here = dot(left_side[:count], right_side, 1, right_dim) + swap(away, "core").astype(F32)
    width = here.shape[1]
    half = width // 2
    here = here.reshape(2, 2, count // 4, width)
    left, right = here[..., :half], here[..., half:]
    left_y = swap(left[1].astype(LOW), "y")
    right_x = swap(right[:, 1].astype(LOW), "tensor")
    left = left[0] + left_y.astype(F32)
    right = right[:, 0] + right_x.astype(F32)
    left_x = swap(left[1].astype(LOW), "tensor")
    right_y = swap(right[1].astype(LOW), "y")
    left = left[0] + left_x.astype(F32)
    right = right[0] + right_y.astype(F32)
    return jnp.concatenate([left, right], axis=-1)


def spread_weights(block, y_at, core_at):
    rows, _, width = block.shape
    block = block.reshape(rows, 2, 2, width)
    other = swap(pick(block, 1 - y_at, 1), "y")
    block = in_order(pick(block, y_at, 1), other, y_at)
    other = swap(pick(block, 1 - core_at, 2), "core")
    block = in_order(pick(block, core_at, 2), other, core_at)
    block = jnp.swapaxes(block, 0, 1).reshape(4 * rows, width)
    return lax.all_gather(block, "z", axis=0, tiled=True)


def sum_weights(block, y_at, core_at):
    block = lax.psum_scatter(block, "z", scatter_dimension=0, tiled=True)
    width = block.shape[1]
    block = block.reshape(2, 2, -1, width)
    other = swap(pick(block, 1 - core_at, 1), "core")
    block = in_order(pick(block, core_at, 1), other, core_at)
    other = swap(pick(block, 1 - y_at, 1), "y")
    block = in_order(pick(block, y_at, 1), other, y_at)
    block = block.reshape(4, -1, width)
    return jnp.swapaxes(block, 0, 1)


def sum_all(block, sizes):
    for axis, size in sizes:
        step = 1
        while step < size:
            block = block + lax.ppermute(block, axis, [(i, i ^ step) for i in range(size)])
            step *= 2
    return block


def quarters(block, width):
    rows = block.shape[0]
    block = block.reshape(rows, 4, -1)
    return jnp.pad(block, ((0, 0), (0, 0), (0, width - block.shape[2])))


def local(
    tokens,
    segment_ids,
    cotangent,
    w_qkv,
    m_qkv,
    v_qkv,
    w_out,
    m_out,
    v_out,
    w_gate_up,
    m_gate_up,
    v_gate_up,
    w_down,
    m_down,
    v_down,
    b_qkv,
    m_bias,
    v_bias,
    ln_params,
    m_norm,
    v_norm,
):
    share, model_width = tokens.shape
    length = segment_ids.shape[1]
    half_heads = b_qkv.shape[1]
    own_heads = half_heads // 4
    heads = own_heads // HD
    half_units = w_down.shape[0]
    own_units = half_units // 4
    units = (own_units + 127) // 128 * 128
    z_size = lax.axis_size("z")
    y_at = lax.axis_index("y")
    core_at = lax.axis_index("core")
    x_at = lax.axis_index("tensor")
    quarter_at = y_at * 2 + core_at
    score_scale = HD ** (-0.5)

    w_out_t = w_out.astype(LOW).T
    w_qkv_low = w_qkv.astype(LOW)
    attn_block = jnp.concatenate(
        [quarters(w_qkv_low[k], own_heads) for k in range(3)] + [quarters(w_out_t, own_heads)],
        axis=2,
    )
    gate_up_low = w_gate_up.astype(LOW)
    gate_up_block = jnp.concatenate([quarters(gate_up_low[k], units) for k in range(2)], axis=2)
    down_block = quarters(w_down.astype(LOW).T, units)

    attn_full = spread_weights(attn_block, y_at, core_at)
    gate_up_full = spread_weights(gate_up_block, y_at, core_at)
    down_full = spread_weights(down_block, y_at, core_at)
    qkv_full = attn_full[:, : 3 * own_heads]
    out_full = attn_full[:, 3 * own_heads :]

    half_places = jnp.arange(share, dtype=jnp.int32)
    positions = jnp.concatenate([half_places + share * x_at, half_places + share * (1 - x_at)])
    cos_part, sin_part = angles(positions)
    ids = segment_ids[0]
    ids = jnp.where(x_at == 0, ids, jnp.concatenate([ids[share:], ids[:share]]))
    ids = jnp.stack([ids, swap(ids, "y")])
    ids = jnp.stack([ids, swap(ids, "core")]).reshape(4, length)
    allowed = (positions[None, :] <= positions[:, None])[None] & (
        ids[:, None, :] == ids[:, :, None]
    )

    inputs_f = tokens.astype(F32)
    hat_a, scale_a = norm_stats(inputs_f)
    a_low = gather_rows((hat_a * ln_params[0] + ln_params[1]).astype(LOW))
    bias = lax.dynamic_slice_in_dim(b_qkv, quarter_at * own_heads, own_heads, 1)
    projected = dot(a_low, qkv_full, 1, 0) + bias.reshape(-1)
    split_heads = projected.reshape(4, length, 3, heads, HD)
    queries = rotate(split_heads[:, :, 0], cos_part, sin_part).astype(LOW)
    key_rows = rotate(split_heads[:, :, 1], cos_part, sin_part).astype(LOW)
    values = split_heads[:, :, 2].astype(LOW)

    def attend_scores():
        scored = (
            jnp.einsum("sqhd,skhd->shqk", queries, key_rows, preferred_element_type=F32)
            * score_scale
        )
        return jnp.where(allowed[:, None], scored, NEG_FILL)

    masked = attend_scores()
    peak_score = jnp.max(masked, axis=-1, keepdims=True)
    exponent = jnp.exp(masked - peak_score)
    totals = jnp.sum(exponent, axis=-1, keepdims=True)
    probs_low = (exponent / totals).astype(LOW)
    log_total = peak_score + jnp.log(totals)
    mixture = jnp.einsum("shqk,skhd->sqhd", probs_low, values, preferred_element_type=F32)
    mixture_low = mixture.reshape(4 * length, own_heads).astype(LOW)
    middle = inputs_f + reduce_rows(mixture_low, out_full, 1)
    hat_c, scale_c = norm_stats(middle)
    c_low = gather_rows((hat_c * ln_params[2] + ln_params[3]).astype(LOW))
    gate_up = dot(c_low, gate_up_full, 1, 0)
    gate, up = gate_up[:, :units], gate_up[:, units:]
    sigma = 1.0 / (1.0 + jnp.exp(-gate))
    hidden_low = (gate * sigma * up).astype(LOW)
    cot_rows = gather_rows(cotangent)
    grad_down = dot(cot_rows, hidden_low, 0, 0).astype(LOW)
    down_sum = sum_weights(grad_down, y_at, core_at)
    d_hidden = dot(cot_rows, down_full, 1, 0)
    d_gate = d_hidden * up * sigma * (1.0 + gate * (1.0 - sigma))
    d_up = d_hidden * (gate * sigma)
    d_gate_up = jnp.concatenate([d_gate, d_up], axis=1).astype(LOW)
    grad_gate_up = dot(c_low, d_gate_up, 0, 0).astype(LOW)
    gate_up_sum = sum_weights(grad_gate_up, y_at, core_at)
    d_normed_c = reduce_rows(d_gate_up, gate_up_full, 1)
    output = (middle + reduce_rows(hidden_low, down_full, 1)).astype(LOW)

    d_middle_n, d_gain_c, d_shift_c = norm_back(hat_c, scale_c, ln_params[2], d_normed_c)
    d_middle = cotangent.astype(F32) + d_middle_n
    branch_rows = gather_rows(d_middle.astype(LOW))
    grad_out = dot(branch_rows, mixture_low, 0, 0).astype(LOW)
    d_mixture = dot(branch_rows, out_full, 1, 0).astype(LOW).reshape(4, length, heads, HD)
    weights_f = jnp.exp(attend_scores() - log_total)
    probs_again = weights_f.astype(LOW)
    d_values = jnp.einsum("shqk,sqhd->skhd", probs_again, d_mixture, preferred_element_type=F32)
    d_weights = jnp.einsum("sqhd,skhd->shqk", d_mixture, values, preferred_element_type=F32)
    d_scores = (
        weights_f * (d_weights - jnp.sum(weights_f * d_weights, axis=-1, keepdims=True))
    ).astype(LOW)
    d_queries = (
        jnp.einsum("shqk,skhd->sqhd", d_scores, key_rows, preferred_element_type=F32) * score_scale
    )
    d_keys = (
        jnp.einsum("shqk,sqhd->skhd", d_scores, queries, preferred_element_type=F32) * score_scale
    )
    d_projected = (
        jnp.stack(
            [
                rotate(d_queries, cos_part, -sin_part),
                rotate(d_keys, cos_part, -sin_part),
                d_values,
            ],
            axis=2,
        )
        .astype(LOW)
        .reshape(4 * length, 3 * own_heads)
    )
    grad_qkv = dot(a_low, d_projected, 0, 0).astype(LOW)
    attn_sum = sum_weights(jnp.concatenate([grad_qkv, grad_out], axis=1), y_at, core_at)
    d_normed_a = reduce_rows(d_projected, qkv_full, 1)
    d_input_n, d_gain_a, d_shift_a = norm_back(hat_a, scale_a, ln_params[0], d_normed_a)
    input_grad = d_middle + d_input_n

    bias_part = jnp.sum(d_projected.astype(F32), axis=0).reshape(3, own_heads)
    bias_part = sum_all(bias_part, (("z", z_size),))
    bias_part = in_order(bias_part, swap(bias_part, "core"), core_at)
    bias_part = in_order(bias_part, swap(bias_part, "y"), y_at)
    bias_grad = jnp.moveaxis(bias_part.reshape(4, 3, own_heads), 0, 1).reshape(3, half_heads)
    norm_part = jnp.stack([d_gain_a, d_shift_a, d_gain_c, d_shift_c])
    norm_grad = sum_all(norm_part, (("core", 2), ("tensor", 2), ("y", 2), ("z", z_size)))

    attn_sum = attn_sum.astype(F32)
    rows = attn_sum.shape[0]
    qkv_grad = jnp.stack(
        [
            attn_sum[:, :, k * own_heads : (k + 1) * own_heads].reshape(rows, half_heads)
            for k in range(3)
        ]
    )
    out_grad = attn_sum[:, :, 3 * own_heads :].reshape(rows, half_heads).T
    gate_up_sum = gate_up_sum.astype(F32)
    gate_up_grad = jnp.stack(
        [
            gate_up_sum[:, :, k * units : k * units + own_units].reshape(rows, half_units)
            for k in range(2)
        ]
    )
    down_grad = down_sum.astype(F32)[:, :, :own_units].reshape(rows, half_units).T

    m_qkv_new, v_qkv_new, w_qkv_new = adamw_update(
        w_qkv, m_qkv, v_qkv, qkv_grad, RATE_MATRIX, DECAY_MATRIX
    )
    m_out_new, v_out_new, w_out_new = adamw_update(
        w_out, m_out, v_out, out_grad, RATE_OUT, DECAY_MATRIX
    )
    m_gate_up_new, v_gate_up_new, w_gate_up_new = adamw_update(
        w_gate_up, m_gate_up, v_gate_up, gate_up_grad, RATE_MATRIX, DECAY_MATRIX
    )
    m_down_new, v_down_new, w_down_new = adamw_update(
        w_down, m_down, v_down, down_grad, RATE_MATRIX, DECAY_MATRIX
    )
    m_bias_new, v_bias_new, b_qkv_new = adamw_update(
        b_qkv, m_bias, v_bias, bias_grad, RATE_SMALL, 0.0
    )
    m_norm_new, v_norm_new, ln_params_new = adamw_update(
        ln_params, m_norm, v_norm, norm_grad, RATE_SMALL, 0.0
    )
    return (
        output,
        input_grad,
        m_qkv_new,
        v_qkv_new,
        w_qkv_new,
        m_out_new,
        v_out_new,
        w_out_new,
        m_gate_up_new,
        v_gate_up_new,
        w_gate_up_new,
        m_down_new,
        v_down_new,
        w_down_new,
        m_bias_new,
        v_bias_new,
        b_qkv_new,
        m_norm_new,
        v_norm_new,
        ln_params_new,
    )


def solution(mesh):
    owners = mesh.shape["dp"]
    pair = mesh.shape["tensor"]
    cut = Mesh(mesh.devices.reshape(owners // 4, 2, 2, pair), ("z", "y", "core", "tensor"))
    dp = ("z", "y", "core")
    rows = P((*dp, "tensor"), None)
    stacked = P(None, dp, "tensor")
    flat = P("tensor", dp)
    bias = P(None, "tensor")
    in_specs = (
        (rows, P(dp, None), rows)
        + (stacked,) * 3
        + (flat,) * 3
        + (stacked,) * 3
        + (flat,) * 3
        + (bias,) * 3
        + (P(),) * 3
    )
    out_specs = (
        (rows, rows)
        + (stacked,) * 3
        + (flat,) * 3
        + (stacked,) * 3
        + (flat,) * 3
        + (bias,) * 3
        + (P(),) * 3
    )
    return jax.shard_map(local, mesh=cut, in_specs=in_specs, out_specs=out_specs, check_vma=False)
```

```python
import functools

import jax
import jax.numpy as jnp
from jax import lax
from jax.experimental import pallas as pl
from jax.experimental.pallas import tpu as pltpu
from jax.sharding import Mesh
from jax.sharding import PartitionSpec as P

HD = 64
ROT = 16
STEP_COUNT = 10

EPS = 1e-05
NEG_FILL = -1000000000.0
BETA_ONE = 0.9
BETA_TWO = 0.95
ADAM_EPS = 1e-08
RATE_MATRIX = 0.01
RATE_OUT = 0.05
RATE_SMALL = 0.25
DECAY_MATRIX = 0.1

LOW = jnp.bfloat16
F32 = jnp.float32
LANES = 128
KERNEL_BYTES = 48 * 2**20


def dot(left, right, left_dim, right_dim):
    return lax.dot_general(
        left, right, (((left_dim,), (right_dim,)), ((), ())), preferred_element_type=F32
    )


def swap(block, axis):
    return lax.ppermute(block, axis, [(0, 1), (1, 0)])


def pick(block, index, dim):
    return lax.dynamic_index_in_dim(block, index, dim, keepdims=False)


def in_order(own, other, index):
    first = index == 0
    return jnp.stack([jnp.where(first, own, other), jnp.where(first, other, own)])


def norm_stats(row_data):
    average = jnp.mean(row_data, axis=-1, keepdims=True)
    centered = row_data - average
    variance = jnp.mean(centered * centered, axis=-1, keepdims=True)
    scale = lax.rsqrt(variance + EPS)
    return centered * scale, scale


def norm_back(hat, scale, gain_vec, grad):
    scaled = grad * gain_vec
    row_grad = (
        scaled
        - jnp.mean(scaled, axis=-1, keepdims=True)
        - hat * jnp.mean(scaled * hat, axis=-1, keepdims=True)
    ) * scale
    return row_grad, jnp.sum(grad * hat, axis=0), jnp.sum(grad, axis=0)


def angle_tables(positions):
    half_rot = ROT // 2
    frequency = 10000.0 ** (-2.0 * jnp.arange(half_rot, dtype=jnp.int32).astype(F32) / ROT)
    angle_table = positions.astype(F32)[:, None] * frequency[None, :]
    cos_part, sin_part = jnp.cos(angle_table), jnp.sin(angle_table)
    rest = jnp.zeros((positions.shape[0], HD - ROT), F32)
    none = jnp.zeros_like(sin_part)

    def table(*parts):
        return jnp.tile(jnp.concatenate(parts, axis=1), (1, LANES // HD))

    return (
        table(cos_part, cos_part, rest + 1.0),
        table(-sin_part, none, rest),
        table(none, sin_part, rest),
    )


def adamw_update(weight, first_mom, second, gradient, step_rate, decay_rate):
    first_mom = BETA_ONE * first_mom + (1.0 - BETA_ONE) * gradient
    second = BETA_TWO * second + (1.0 - BETA_TWO) * gradient * gradient
    fix_first = 1.0 - BETA_ONE**STEP_COUNT
    fix_second = 1.0 - BETA_TWO**STEP_COUNT
    update = first_mom / fix_first / (jnp.sqrt(second / fix_second) + ADAM_EPS)
    return (first_mom, second, weight - step_rate * (update + decay_rate * weight))


def turn(block, cos_t, low_t, high_t):
    return block * cos_t + pltpu.roll(block, LANES - ROT // 2, 1) * low_t + pltpu.roll(block, ROT // 2, 1) * high_t

def assemble(upper_ref, upper_far_ref, lower_ref, lower_far_ref, rows_ref):
    half = lower_ref.shape[1]

    @pl.when(pl.program_id(0) == 0)
    def near():
        rows_ref[: 2 * half] = upper_ref[...].reshape(2 * half, -1)

    @pl.when(pl.program_id(0) == 1)
    def far():
        rows_ref[: 2 * half] = upper_far_ref[...].reshape(2 * half, -1)

    rows_ref[2 * half : 3 * half] = lower_ref[0]
    rows_ref[3 * half :] = lower_far_ref[0]


def forward_kernel(
    own,
    upper_ref,
    upper_far_ref,
    lower_ref,
    lower_far_ref,
    weight_ref,
    bias_ref,
    cos_ref,
    low_ref,
    high_ref,
    row_ref,
    column_ref,
    rows_ref,
    keep_ref,
    mix_ref,
    branch_ref,
):
    assemble(upper_ref, upper_far_ref, lower_ref, lower_far_ref, rows_ref)
    rows = rows_ref[...]
    length = rows.shape[0]
    cos_t, low_t, high_t = cos_ref[...], low_ref[...], high_ref[...]
    allowed = (row_ref[0, 0:1] <= column_ref[0, :, 0:1]) & (
        row_ref[0, 1:2] == column_ref[0, :, 1:2]
    )
    first_head = lax.broadcasted_iota(jnp.int32, (length, LANES), 1) < HD
    scale = HD**-0.5
    for part in range(3):
        cols = slice(part * own, (part + 1) * own)
        made = dot(rows, weight_ref[:, cols], 1, 0) + bias_ref[:, cols]
        for at in range(0, own, LANES):
            piece = made[:, at : at + LANES]
            if part < 2:
                piece = turn(piece, cos_t, low_t, high_t)
            keep_ref[:, part * own + at : part * own + at + LANES] = piece.astype(LOW)
    for at in range(0, own, LANES):
        q2 = keep_ref[:, at : at + LANES]
        k2 = keep_ref[:, own + at : own + at + LANES]
        v2 = keep_ref[:, 2 * own + at : 2 * own + at + LANES]
        outs = []
        for head in range(2):
            mine = first_head if head == 0 else ~first_head
            scored = dot(jnp.where(mine, q2, jnp.zeros_like(q2)), k2, 1, 1) * scale
            scored = jnp.where(allowed, scored, NEG_FILL)
            exponent = jnp.exp(scored - jnp.max(scored, axis=1, keepdims=True))
            total = jnp.sum(exponent, axis=1, keepdims=True)
            outs.append(dot((exponent * (1.0 / total)).astype(LOW), v2, 1, 0))
        mix_ref[:, at : at + LANES] = jnp.where(first_head, outs[0], outs[1]).astype(LOW)
    branch_ref[...] = dot(mix_ref[...], weight_ref[:, 3 * own :], 1, 1).astype(branch_ref.dtype)


def backward_kernel(
    own,
    upper_ref,
    upper_far_ref,
    lower_ref,
    lower_far_ref,
    weight_ref,
    keep_ref,
    cos_ref,
    low_ref,
    high_ref,
    row_ref,
    column_ref,
    rows_ref,
    grad_ref,
    normed_ref,
):
    assemble(upper_ref, upper_far_ref, lower_ref, lower_far_ref, rows_ref)
    length = rows_ref.shape[0]
    cos_t, low_t, high_t = cos_ref[...], -low_ref[...], -high_ref[...]
    allowed = (column_ref[0, :, 0:1] <= row_ref[0, 0:1]) & (
        row_ref[0, 1:2] == column_ref[0, :, 1:2]
    )
    first_head = lax.broadcasted_iota(jnp.int32, (length, LANES), 1) < HD
    scale = HD**-0.5
    d_mix = dot(rows_ref[...], weight_ref[:, 3 * own :], 1, 0).astype(LOW)
    for at in range(0, own, LANES):
        q2 = keep_ref[:, at : at + LANES]
        k2 = keep_ref[:, own + at : own + at + LANES]
        v2 = keep_ref[:, 2 * own + at : 2 * own + at + LANES]
        do2 = d_mix[:, at : at + LANES]
        dq, dk, dv = [], [], []
        for head in range(2):
            mine = first_head if head == 0 else ~first_head
            scored = dot(jnp.where(mine, k2, jnp.zeros_like(k2)), q2, 1, 1) * scale
            scored = jnp.where(allowed, scored, NEG_FILL)
            exponent = jnp.exp(scored - jnp.max(scored, axis=0, keepdims=True))
            weights = exponent * (1.0 / jnp.sum(exponent, axis=0, keepdims=True))
            d_weights = dot(jnp.where(mine, v2, jnp.zeros_like(v2)), do2, 1, 1)
            total = jnp.sum(weights * d_weights, axis=0, keepdims=True)
            d_scores = (weights * (d_weights - total)).astype(LOW)
            dv.append(dot(weights.astype(LOW), do2, 1, 0))
            dk.append(dot(d_scores, q2, 1, 0))
            dq.append(dot(d_scores, k2, 0, 0))
        for part, pair in enumerate((dq, dk, dv)):
            piece = jnp.where(first_head, pair[0], pair[1])
            if part < 2:
                piece = turn(piece * scale, cos_t, low_t, high_t)
            grad_ref[:, part * own + at : part * own + at + LANES] = piece.astype(LOW)
    normed_ref[...] = dot(grad_ref[...], weight_ref[:, : 3 * own], 1, 1).astype(normed_ref.dtype)


def both_halves(block, first_half):
    other = pltpu.roll(block, LANES // 2, 1)
    return jnp.where(first_half, block, other), jnp.where(first_half, other, block)


def mlp_kernel(
    main,
    upper_ref,
    upper_far_ref,
    lower_ref,
    lower_far_ref,
    weight_ref,
    rows_ref,
    gate_up_ref,
    hidden_ref,
):
    assemble(upper_ref, upper_far_ref, lower_ref, lower_far_ref, rows_ref)
    rows = rows_ref[...]
    for at in range(0, 2 * main + LANES, 2 * LANES):
        cols = slice(at, min(at + 2 * LANES, 2 * main + LANES))
        gate_up_ref[:, cols] = dot(rows, weight_ref[:, cols], 1, 0)
    for at in range(0, main, LANES):
        gate = gate_up_ref[:, at : at + LANES]
        up = gate_up_ref[:, main + at : main + at + LANES]
        hidden_ref[:, at : at + LANES] = (gate / (1.0 + jnp.exp(-gate)) * up).astype(LOW)
    last = gate_up_ref[:, 2 * main :]
    first_half = lax.broadcasted_iota(jnp.int32, last.shape, 1) < LANES // 2
    gate, up = both_halves(last, first_half)
    made = gate / (1.0 + jnp.exp(-gate)) * up
    hidden_ref[:, main:] = jnp.where(first_half, made, 0.0).astype(LOW)


def gate_up_back(gate, up, d_hidden):
    sigma = 1.0 / (1.0 + jnp.exp(-gate))
    d_gate = d_hidden * up * sigma * (1.0 + gate * (1.0 - sigma))
    return d_gate.astype(LOW), (d_hidden * (gate * sigma)).astype(LOW)


def mlp_back_kernel(main, rows_ref, down_ref, gate_up_ref, grad_ref):
    rows = rows_ref[...]
    for start in range(0, main + LANES, 2 * LANES):
        d_hidden = dot(rows, down_ref[:, start : start + 2 * LANES], 1, 0)
        for at in range(start, min(start + 2 * LANES, main), LANES):
            d_gate, d_up = gate_up_back(
                gate_up_ref[:, at : at + LANES],
                gate_up_ref[:, main + at : main + at + LANES],
                d_hidden[:, at - start : at - start + LANES],
            )
            grad_ref[:, at : at + LANES] = d_gate
            grad_ref[:, main + at : main + at + LANES] = d_up
    last = gate_up_ref[:, 2 * main :]
    first_half = lax.broadcasted_iota(jnp.int32, last.shape, 1) < LANES // 2
    gate, up = both_halves(last, first_half)
    d_hidden, _ = both_halves(d_hidden[:, main - start :], first_half)
    d_gate, d_up = gate_up_back(gate, up, d_hidden)
    grad_ref[:, 2 * main :] = jnp.where(first_half, d_gate, d_up)


def mlp_back_send_kernel(main, rows_ref, down_ref, weight_ref, gate_up_ref, grad_ref, sent_ref):
    mlp_back_kernel(main, rows_ref, down_ref, gate_up_ref, grad_ref)
    sent_ref[...] = dot(grad_ref[...], weight_ref[...], 1, 1).astype(LOW)


def add_kernel(
    left_ref, right_ref, got_ref, upper_sent_ref, lower_sent_ref, upper_ref, lower_ref
):
    total = dot(left_ref[...], right_ref[...], 1, 1) + got_ref[...].astype(F32)
    half = lower_ref.shape[1]

    @pl.when(pl.program_id(0) == 0)
    def near():
        upper_ref[...] = total[: 2 * half].reshape(2, half, -1)

    @pl.when(pl.program_id(0) == 1)
    def far():
        upper_sent_ref[...] = total[: 2 * half].reshape(2, half, -1).astype(LOW)

    lower_ref[0] = total[2 * half : 3 * half]
    lower_sent_ref[0] = total[3 * half :].astype(LOW)


def whole(shape):
    return pl.BlockSpec(shape, lambda i: (0,) * len(shape))


HELD = pl.BlockSpec(memory_space=pltpu.VMEM)


def sequences(length, width, first=0):
    return pl.BlockSpec((length, width), lambda i: (first + i, 0))


def piece_specs(pieces):
    upper, _, lower, _ = pieces
    moving = pl.BlockSpec((1, *lower.shape[1:]), lambda i: (i, 0, 0))
    return [whole(upper.shape), whole(upper.shape), moving, moving]


def info_specs(length, first):
    return [
        pl.BlockSpec((1, 2, length), lambda i: (first + i, 0, 0)),
        pl.BlockSpec((1, length, 2), lambda i: (first + i, 0, 0)),
    ]


def call(kernel, in_specs, out_specs, out_shape, flops, operands):
    return pl.pallas_call(
        kernel,
        grid=(2,),
        in_specs=in_specs,
        out_specs=out_specs,
        out_shape=[jax.ShapeDtypeStruct(*item) for item in out_shape],
        compiler_params=pltpu.CompilerParams(vmem_limit_bytes=KERNEL_BYTES),
        cost_estimate=pl.CostEstimate(flops=flops, bytes_accessed=0, transcendentals=0),
    )(*operands)


def collect(pieces, length):
    width = pieces[0].shape[2]
    return call(
        assemble,
        piece_specs(pieces),
        [sequences(length, width)],
        [((2 * length, width), LOW)],
        0,
        pieces,
    )[0]


def attend(pieces, weight, bias, tables, row_info, column_info, first, kind):
    length = row_info.shape[2]
    count = 2 * length
    width = weight.shape[0]
    own = weight.shape[1] // 4
    return call(
        functools.partial(forward_kernel, own),
        piece_specs(pieces)
        + [whole(weight.shape), whole(bias.shape)]
        + [whole(table.shape) for table in tables]
        + info_specs(length, first),
        [sequences(length, item) for item in (width, 3 * own, own, width)],
        [
            ((count, width), LOW),
            ((count, 3 * own), LOW),
            ((count, own), LOW),
            ((count, width), kind),
        ],
        2 * count * (width * 4 * own + 4 * length * own),
        (*pieces, weight, bias, *tables, row_info, column_info),
    )


def attend_back(pieces, weight, kept, tables, row_info, column_info, first, kind):
    length = row_info.shape[2]
    count = 2 * length
    width = weight.shape[0]
    own = weight.shape[1] // 4
    return call(
        functools.partial(backward_kernel, own),
        piece_specs(pieces)
        + [whole(weight.shape), sequences(length, 3 * own)]
        + [whole(table.shape) for table in tables]
        + info_specs(length, first),
        [sequences(length, item) for item in (width, 3 * own, width)],
        [((count, width), LOW), ((count, 3 * own), LOW), ((count, width), kind)],
        2 * count * (width * 4 * own + 10 * length * own),
        (*pieces, weight, kept, *tables, row_info, column_info),
    )


def mlp(pieces, weight, length):
    count = 2 * length
    width, both = weight.shape
    main = (both - LANES) // 2
    return call(
        functools.partial(mlp_kernel, main),
        piece_specs(pieces) + [whole(weight.shape)],
        [sequences(length, item) for item in (width, both, main + LANES)],
        [((count, width), LOW), ((count, both), F32), ((count, main + LANES), LOW)],
        2 * count * width * both,
        (*pieces, weight),
    )


def mlp_back(rows, down, gate_up, length, weight=None):
    count = 2 * length
    width = rows.shape[1]
    both = gate_up.shape[1]
    specs = [sequences(length, width), HELD, sequences(length, both)]
    operands = [rows, down, gate_up]
    kernel, widths = mlp_back_kernel, (both,)
    if weight is not None:
        specs.insert(2, HELD)
        operands.insert(2, weight)
        kernel, widths = mlp_back_send_kernel, (both, width)
    return call(
        functools.partial(kernel, (both - LANES) // 2),
        specs,
        [sequences(length, item) for item in widths],
        [((count, item), LOW) for item in widths],
        (2 * len(widths) - 1) * count * width * both,
        operands,
    )


def add_rows(left, right, got, length):
    half = length // 4
    width = right.shape[0]
    shape = (2, half, width)
    moving = pl.BlockSpec((1, half, width), lambda i: (i, 0, 0))
    return call(
        add_kernel,
        [sequences(length, left.shape[1]), HELD, sequences(length, width)],
        [whole(shape), moving, whole(shape), moving],
        [(shape, LOW), (shape, LOW), (shape, F32), (shape, F32)],
        4 * length * width * left.shape[1],
        (left, right, got),
    )


def grads_kernel(widths, *refs):
    out_ref = refs[-1]
    at = 0
    for k, width in enumerate(widths):
        left_here, left_away, right_here, right_away = refs[4 * k : 4 * k + 4]
        made = dot(left_here[...], right_here[...], 0, 0) + dot(
            left_away[...], right_away[...], 0, 0
        )
        out_ref[:, at : at + width] = made.astype(LOW)
        at += width


def grads(*parts):
    operands, specs, widths, flops = [], [], [], 0
    for lefts, rights in parts:
        count, width = rights[0].shape
        depth = lefts[0].shape[1]
        block = min(512, depth)
        for half, left in enumerate(lefts):
            row = half if left.shape[0] == 2 * count else 0
            specs.append(pl.BlockSpec((count, block), lambda i, row=row: (row, i)))
        specs += [whole(right.shape) for right in rights]
        operands += [*lefts, *rights]
        widths.append(width)
        flops += 4 * count * depth * width
    total = sum(widths)
    return pl.pallas_call(
        functools.partial(grads_kernel, tuple(widths)),
        grid=(depth // block,),
        in_specs=specs,
        out_specs=pl.BlockSpec((block, total), lambda i: (i, 0)),
        out_shape=jax.ShapeDtypeStruct((depth, total), LOW),
        compiler_params=pltpu.CompilerParams(vmem_limit_bytes=KERNEL_BYTES),
        cost_estimate=pl.CostEstimate(flops=flops, bytes_accessed=0, transcendentals=0),
    )(*operands)


def adamw_write(refs, index, gradient, step_rate, decay_rate):
    weight, first_mom, second, new_first, new_second, new_weight = refs
    made = adamw_update(
        weight[index], first_mom[index], second[index], gradient, step_rate, decay_rate
    )
    new_first[index], new_second[index], new_weight[index] = made


def piece_of(at_ref, near_ref, far_ref, quarter, cols):
    y_away = lax.rem(quarter // 2 + at_ref[0], 2)
    core_away = lax.rem(lax.rem(quarter, 2) + at_ref[1], 2)
    near = near_ref[core_away, :, cols]
    return jnp.where(y_away == 0, near, far_ref[core_away, :, cols]).astype(F32)


def attn_update_kernel(own, at_ref, near_ref, far_ref, *refs):
    quarter = pl.program_id(0)
    qkv, out = refs[0:3] + refs[6:9], refs[3:6] + refs[9:12]
    for part in range(3):
        cols = slice(part * own, (part + 1) * own)
        gradient = piece_of(at_ref, near_ref, far_ref, quarter, cols)
        adamw_write(qkv, part, gradient, RATE_MATRIX, DECAY_MATRIX)
    gradient = piece_of(at_ref, near_ref, far_ref, quarter, slice(3 * own, 4 * own))
    adamw_write(out, slice(None), gradient.T, RATE_OUT, DECAY_MATRIX)


def gate_up_update_kernel(main, at_ref, near_ref, far_ref, *refs):
    part = pl.program_id(0)
    rows = near_ref.shape[1]
    first_half = lax.broadcasted_iota(jnp.int32, (rows, LANES), 1) < LANES // 2
    tails = []
    for quarter in range(4):
        cols = pl.ds(pl.multiple_of(part * main, LANES), main)
        gradient = piece_of(at_ref, near_ref, far_ref, quarter, cols)
        index = (0, slice(None), slice(quarter * main, (quarter + 1) * main))
        adamw_write(refs, index, gradient, RATE_MATRIX, DECAY_MATRIX)
        last = piece_of(at_ref, near_ref, far_ref, quarter, slice(2 * main, 2 * main + LANES))
        tails.append((last, pltpu.roll(last, LANES // 2, 1)))
    for pair in range(2):
        (left, left_turned), (right, right_turned) = tails[2 * pair : 2 * pair + 2]
        left = jnp.where(part == 0, left, left_turned)
        right = jnp.where(part == 0, right_turned, right)
        at = 4 * main + pair * LANES
        index = (0, slice(None), slice(at, at + LANES))
        adamw_write(
            refs, index, jnp.where(first_half, left, right), RATE_MATRIX, DECAY_MATRIX
        )


def down_update_kernel(main, at_ref, near_ref, far_ref, *refs):
    for quarter in range(4):
        gradient = piece_of(at_ref, near_ref, far_ref, quarter, slice(0, main + LANES)).T
        for source, at, size in (
            (0, quarter * main, main),
            (main, 4 * main + quarter * (LANES // 2), LANES // 2),
        ):
            adamw_write(
                refs,
                slice(at, at + size),
                gradient[source : source + size],
                RATE_MATRIX,
                DECAY_MATRIX,
            )


def update(kernel, steps, specs, places, pieces, arrays):
    near, far = pieces
    return pl.pallas_call(
        kernel,
        grid_spec=pltpu.PrefetchScalarGridSpec(
            num_scalar_prefetch=1,
            grid=(steps,),
            in_specs=[pl.BlockSpec(near.shape, lambda i, at: (0, 0, 0))] * 2 + specs,
            out_specs=specs,
        ),
        out_shape=[jax.ShapeDtypeStruct(array.shape, F32) for array in arrays],
        compiler_params=pltpu.CompilerParams(vmem_limit_bytes=KERNEL_BYTES),
        cost_estimate=pl.CostEstimate(
            flops=0, bytes_accessed=24 * sum(array.size for array in arrays) // 3, transcendentals=0
        ),
    )(places, near, far, *arrays)


def gather_start(rows):
    half = rows.shape[0] // 2
    upper, lower = rows[:half], rows[half:]
    return upper, swap(upper, "tensor"), lower, swap(lower, "y")


def gather_end(upper, upper_x, lower, lower_y):
    upper_pair = jnp.stack([upper, upper_x])
    lower_pair = jnp.stack([lower, lower_y])
    here = (upper_pair, swap(upper_pair, "y"), lower_pair, swap(lower_pair, "tensor"))
    return here, tuple(swap(piece, "core") for piece in here)


def gather_rows(rows):
    return gather_end(*gather_start(rows))


def reduce_start(here, away):
    away = swap(away, "core")
    total = (here.astype(F32) + away.astype(F32)).reshape(2, 2, 2, -1, here.shape[1])
    upper, lower = total[:, 0], total[:, 1]
    return upper[1].astype(LOW), lower[:, 1].astype(LOW), upper[0], lower[:, 0]


def reduce_first(upper_sent, lower_sent, upper, lower):
    return upper, swap(upper_sent, "y"), lower, swap(lower_sent, "tensor")


def reduce_second(upper, upper_got, lower, lower_got):
    upper = upper + upper_got.astype(F32)
    lower = lower + lower_got.astype(F32)
    return (
        upper[0],
        swap(upper[1].astype(LOW), "tensor"),
        lower[0],
        swap(lower[1].astype(LOW), "y"),
    )


def reduce_end(upper, upper_got, lower, lower_got):
    return jnp.concatenate(
        [upper + upper_got.astype(F32), lower + lower_got.astype(F32)], axis=0
    )


def reduce_rows(here, away):
    return reduce_end(*reduce_second(*reduce_first(*reduce_start(here, away))))


def tie(*items):
    return lax.optimization_barrier(items)


def spread_y(block, y_at):
    rows, _, width = block.shape
    block = block.reshape(rows, 2, 2, width)
    return in_order(pick(block, y_at, 1), swap(pick(block, 1 - y_at, 1), "y"), y_at)


def spread_core(block, core_at):
    other = swap(pick(block, 1 - core_at, 2), "core")
    block = in_order(pick(block, core_at, 2), other, core_at)
    return jnp.swapaxes(block, 0, 1).reshape(-1, block.shape[-1])


def gather_weights(block):
    return lax.all_gather(block, "z", axis=0, tiled=True)


def sum_weights(block):
    return lax.psum_scatter(block, "z", scatter_dimension=0, tiled=True)


def return_weights(block, y_at, core_at):
    width = block.shape[1]
    block = block.reshape(2, 2, -1, width)
    other = swap(pick(block, 1 - core_at, 1), "core")
    block = jnp.stack([pick(block, core_at, 1), other])
    return pick(block, y_at, 1), swap(pick(block, 1 - y_at, 1), "y")


def sum_all(block, sizes):
    for axis, size in sizes:
        step = 1
        while step < size:
            block = block + lax.ppermute(block, axis, [(i, i ^ step) for i in range(size)])
            step *= 2
    return block


def quarters(block):
    return block.reshape(block.shape[0], 4, -1)


def split_units(block, main):
    return quarters(block[:, : 4 * main]), quarters(block[:, 4 * main :])


def local(
    tokens,
    segment_ids,
    cotangent,
    w_qkv,
    m_qkv,
    v_qkv,
    w_out,
    m_out,
    v_out,
    w_gate_up,
    m_gate_up,
    v_gate_up,
    w_down,
    m_down,
    v_down,
    b_qkv,
    m_bias,
    v_bias,
    ln_params,
    m_norm,
    v_norm,
):
    share, model_width = tokens.shape
    length = segment_ids.shape[1]
    half_heads = b_qkv.shape[1]
    own_heads = half_heads // 4
    half_units = w_down.shape[0]
    main = half_units // 4 // LANES * LANES
    y_at = lax.axis_index("y")
    core_at = lax.axis_index("core")
    x_at = lax.axis_index("tensor")
    z_size = lax.axis_size("z")
    quarter_at = y_at * 2 + core_at

    w_qkv_low = w_qkv.astype(LOW)
    attn_block = jnp.concatenate(
        [quarters(w_qkv_low[k]) for k in range(3)] + [quarters(w_out.astype(LOW).T)], axis=2
    )
    gate_up_low = w_gate_up.astype(LOW)
    gate_main, gate_tail = split_units(gate_up_low[0], main)
    up_main, up_tail = split_units(gate_up_low[1], main)
    gate_up_block = jnp.concatenate([gate_main, up_main, gate_tail, up_tail], axis=2)
    down_main, down_tail = split_units(w_down.astype(LOW).T, main)
    down_block = jnp.concatenate([down_main, down_tail, jnp.zeros_like(down_tail)], axis=2)

    half = share // 2
    places = jnp.arange(half, dtype=jnp.int32)
    x_order = jnp.stack([x_at, 1 - x_at])
    positions = (
        jnp.arange(2, dtype=jnp.int32)[:, None, None] * half
        + x_order[None, :, None] * share
        + places[None, None, :]
    ).reshape(length)
    tables = angle_tables(positions)
    ids = segment_ids[0].reshape(2, 2, half)
    ids = jnp.swapaxes(jnp.where(x_at == 0, ids, ids[::-1]), 0, 1).reshape(length)
    bias = lax.dynamic_slice_in_dim(b_qkv, quarter_at * own_heads, own_heads, 1).reshape(1, -1)

    inputs_f = tokens.astype(F32)
    hat_a, scale_a = norm_stats(inputs_f)
    a_low = (hat_a * ln_params[0] + ln_params[1]).astype(LOW)
    attn_block = spread_core(spread_y(attn_block, y_at), core_at)
    attn_block, a_low, ids, gate_up_block = tie(attn_block, a_low, ids, gate_up_block)
    attn_full = gather_weights(attn_block)
    gate_up_block = spread_y(gate_up_block, y_at)
    ids = jnp.stack([ids, swap(ids, "y")])
    flow, ids, gate_up_block = tie(gather_start(a_low), ids, gate_up_block)
    gate_up_block = spread_core(gate_up_block, core_at)
    ids = jnp.stack([ids, swap(ids, "core")]).reshape(4, length)
    row_info = jnp.stack([jnp.broadcast_to(positions, ids.shape), ids], axis=1)
    column_info = jnp.swapaxes(row_info, 1, 2)
    a_here, a_away = gather_end(*flow)
    a_here, gate_up_block, row_info, column_info, cot_low, down_block = tie(
        a_here, gate_up_block, row_info, column_info, cotangent, down_block
    )
    gate_up_full = gather_weights(gate_up_block)
    flow, down_block, a_here, a_away = tie(
        gather_start(cot_low), spread_y(down_block, y_at), a_here, a_away
    )
    down_block = spread_core(down_block, core_at)
    cot_here, cot_away = gather_end(*flow)
    seq_info = (tables, row_info, column_info)
    a_rows_away, kept_away, mix_away, branch_away = attend(
        a_away, attn_full, bias, *seq_info, 2, LOW
    )
    down_block, cot_here, cot_away, a_here = tie(down_block, cot_here, cot_away, a_here)
    down_full = gather_weights(down_block)
    a_rows_here, kept_here, mix_here, branch_here = attend(
        a_here, attn_full, bias, *seq_info, 0, F32
    )
    flow = reduce_first(*reduce_start(branch_here, branch_away))
    flow, cot_here, cot_away = tie(flow, collect(cot_here, length), collect(cot_away, length))
    middle = inputs_f + reduce_end(*reduce_second(*flow))
    hat_c, scale_c = norm_stats(middle)
    c_here, c_away = gather_rows((hat_c * ln_params[2] + ln_params[3]).astype(LOW))
    c_rows_here, gate_up_here, hidden_here = mlp(c_here, gate_up_full, length)
    c_rows_away, gate_up_away, hidden_away = mlp(c_away, gate_up_full, length)
    grad_down = grads(((cot_here, cot_away), (hidden_here, hidden_away)))
    cot_here, cot_away, grad_down = tie(cot_here, cot_away, grad_down)
    down_sum = sum_weights(grad_down)
    mlp_away, normed_away = mlp_back(cot_away, down_full, gate_up_away, length, gate_up_full)
    (mlp_here,) = mlp_back(cot_here, down_full, gate_up_here, length)
    flow = add_rows(mlp_here, gate_up_full, swap(normed_away, "core"), length)
    flow, mlp_here, mlp_away = tie(flow, mlp_here, mlp_away)
    grad_gate_up = grads(((c_rows_here, c_rows_away), (mlp_here, mlp_away)))
    flow, grad_gate_up, hidden_here, hidden_away = tie(
        reduce_first(*flow), grad_gate_up, hidden_here, hidden_away
    )
    gate_up_sum = sum_weights(grad_gate_up)
    result_away = dot(hidden_away, down_full, 1, 1).astype(LOW)
    flow, result_away, hidden_here = tie(reduce_second(*flow), result_away, hidden_here)
    d_normed_c = reduce_end(*flow)

    d_middle_n, d_gain_c, d_shift_c = norm_back(hat_c, scale_c, ln_params[2], d_normed_c)
    d_middle = cotangent.astype(F32) + d_middle_n
    result = add_rows(hidden_here, down_full, swap(result_away, "core"), length)
    flow, result = tie(gather_start(d_middle.astype(LOW)), result)
    branch_here, branch_away = gather_end(*flow)
    branch_here, result = tie(branch_here, result)
    result = reduce_first(*result)
    b_rows_here, back_here, normed_here = attend_back(
        branch_here, attn_full, kept_here, *seq_info, 0, F32
    )
    down_sum = return_weights(down_sum, y_at, core_at)
    result, branch_away, down_sum = tie(result, branch_away, down_sum)
    result = reduce_second(*result)
    b_rows_away, back_away, normed_away = attend_back(
        branch_away, attn_full, kept_away, *seq_info, 2, LOW
    )
    result, back_away = tie(result, back_away)
    grad_attn = grads(
        ((a_rows_here, a_rows_away), (back_here, back_away)),
        ((b_rows_here, b_rows_away), (mix_here, mix_away)),
    )
    grad_attn, normed_here, normed_away, back_here, back_away, result = tie(
        grad_attn, normed_here, normed_away, back_here, back_away, result
    )
    attn_sum = sum_weights(grad_attn)
    flow = reduce_second(*reduce_first(*reduce_start(normed_here, normed_away)))
    flow, gate_up_sum = tie(flow, gate_up_sum)
    gate_up_sum = return_weights(gate_up_sum, y_at, core_at)
    d_normed_a = reduce_end(*flow)
    output = (middle + reduce_end(*result)).astype(LOW)
    d_input_n, d_gain_a, d_shift_a = norm_back(hat_a, scale_a, ln_params[0], d_normed_a)
    input_grad = d_middle + d_input_n

    bias_part = jnp.sum(back_here.astype(F32), axis=0) + jnp.sum(back_away.astype(F32), axis=0)
    bias_full = lax.dynamic_update_slice_in_dim(
        jnp.zeros((3, model_width), F32),
        bias_part.reshape(3, own_heads),
        x_at * half_heads + quarter_at * own_heads,
        1,
    )
    small = jnp.concatenate(
        [jnp.stack([d_gain_a, d_shift_a, d_gain_c, d_shift_c]), bias_full], axis=0
    )
    small = sum_all(small, (("core", 2), ("tensor", 2), ("z", z_size), ("y", 2)))
    norm_grad = small[:4]
    bias_grad = lax.dynamic_slice_in_dim(small[4:], x_at * half_heads, half_heads, 1)

    m_bias_new, v_bias_new, b_qkv_new = adamw_update(
        b_qkv, m_bias, v_bias, bias_grad, RATE_SMALL, 0.0
    )
    m_norm_new, v_norm_new, ln_params_new = adamw_update(
        ln_params, m_norm, v_norm, norm_grad, RATE_SMALL, 0.0
    )
    bias_new = (m_bias_new, v_bias_new, b_qkv_new)
    norm_new = (m_norm_new, v_norm_new, ln_params_new)
    attn_sum, output, input_grad, bias_new, norm_new, gate_up_sum, down_sum = tie(
        attn_sum, output, input_grad, bias_new, norm_new, gate_up_sum, down_sum
    )
    places = jnp.stack([y_at, core_at]).astype(jnp.int32)
    rows = w_qkv.shape[1]
    stacked = pl.BlockSpec((1, *w_gate_up.shape[1:]), lambda i, at: (i, 0, 0))
    gate_up_new = update(
        functools.partial(gate_up_update_kernel, main),
        2,
        [stacked] * 3,
        places,
        gate_up_sum,
        (w_gate_up, m_gate_up, v_gate_up),
    )
    flat = pl.BlockSpec(w_down.shape, lambda i, at: (0, 0))
    down_new = update(
        functools.partial(down_update_kernel, main),
        1,
        [flat] * 3,
        places,
        down_sum,
        (w_down, m_down, v_down),
    )
    qkv = pl.BlockSpec((3, rows, own_heads), lambda i, at: (0, 0, i))
    out = pl.BlockSpec((own_heads, rows), lambda i, at: (i, 0))
    attn_new = update(
        functools.partial(attn_update_kernel, own_heads),
        4,
        [qkv] * 3 + [out] * 3,
        places,
        return_weights(attn_sum, y_at, core_at),
        (w_qkv, m_qkv, v_qkv, w_out, m_out, v_out),
    )
    return (output, input_grad, *attn_new, *gate_up_new, *down_new, *bias_new, *norm_new)


def solution(mesh):
    owners = mesh.shape["dp"]
    pair = mesh.shape["tensor"]
    cut = Mesh(mesh.devices.reshape(owners // 4, 2, 2, pair), ("z", "y", "core", "tensor"))
    dp = ("z", "y", "core")
    rows = P((*dp, "tensor"), None)
    stacked = P(None, dp, "tensor")
    flat = P("tensor", dp)
    bias = P(None, "tensor")
    in_specs = (
        (rows, P(dp, None), rows)
        + (stacked,) * 3
        + (flat,) * 3
        + (stacked,) * 3
        + (flat,) * 3
        + (bias,) * 3
        + (P(),) * 3
    )
    out_specs = (
        (rows, rows)
        + (stacked,) * 3
        + (flat,) * 3
        + (stacked,) * 3
        + (flat,) * 3
        + (bias,) * 3
        + (P(),) * 3
    )
    return jax.shard_map(local, mesh=cut, in_specs=in_specs, out_specs=out_specs, check_vma=False)
```

```python
import functools

import jax
import jax.numpy as jnp
from jax import lax
from jax.experimental import pallas as pl
from jax.experimental.pallas import tpu as pltpu
from jax.sharding import Mesh
from jax.sharding import PartitionSpec as P

HD = 64
ROT = 16
STEP_COUNT = 10

EPS = 1e-05
NEG_FILL = -1000000000.0
BETA_ONE = 0.9
BETA_TWO = 0.95
ADAM_EPS = 1e-08
RATE_MATRIX = 0.01
RATE_OUT = 0.05
RATE_SMALL = 0.25
DECAY_MATRIX = 0.1

LOW = jnp.bfloat16
F32 = jnp.float32
LANES = 128
KERNEL_BYTES = 48 * 2**20


def dot(left, right, left_dim, right_dim):
    return lax.dot_general(
        left, right, (((left_dim,), (right_dim,)), ((), ())), preferred_element_type=F32
    )


def swap(block, axis):
    return lax.ppermute(block, axis, [(0, 1), (1, 0)])


def pick(block, index, dim):
    return lax.dynamic_index_in_dim(block, index, dim, keepdims=False)


def in_order(own, other, index):
    first = index == 0
    return jnp.stack([jnp.where(first, own, other), jnp.where(first, other, own)])


def norm_stats(row_data):
    average = jnp.mean(row_data, axis=-1, keepdims=True)
    centered = row_data - average
    variance = jnp.mean(centered * centered, axis=-1, keepdims=True)
    scale = lax.rsqrt(variance + EPS)
    return centered * scale, scale


def norm_back(hat, scale, gain_vec, grad):
    scaled = grad * gain_vec
    row_grad = (
        scaled
        - jnp.mean(scaled, axis=-1, keepdims=True)
        - hat * jnp.mean(scaled * hat, axis=-1, keepdims=True)
    ) * scale
    return row_grad, jnp.sum(grad * hat, axis=0), jnp.sum(grad, axis=0)


def angle_tables(positions):
    half_rot = ROT // 2
    frequency = 10000.0 ** (-2.0 * jnp.arange(half_rot, dtype=jnp.int32).astype(F32) / ROT)
    angle_table = positions.astype(F32)[:, None] * frequency[None, :]
    cos_part, sin_part = jnp.cos(angle_table), jnp.sin(angle_table)
    rest = jnp.zeros((positions.shape[0], HD - ROT), F32)
    none = jnp.zeros_like(sin_part)

    def table(*parts):
        return jnp.tile(jnp.concatenate(parts, axis=1), (1, LANES // HD))

    return (
        table(cos_part, cos_part, rest + 1.0),
        table(-sin_part, none, rest),
        table(none, sin_part, rest),
    )


def adamw_update(weight, first_mom, second, gradient, step_rate, decay_rate):
    first_mom = BETA_ONE * first_mom + (1.0 - BETA_ONE) * gradient
    second = BETA_TWO * second + (1.0 - BETA_TWO) * gradient * gradient
    fix_first = 1.0 - BETA_ONE**STEP_COUNT
    fix_second = 1.0 - BETA_TWO**STEP_COUNT
    update = first_mom / fix_first / (jnp.sqrt(second / fix_second) + ADAM_EPS)
    return (first_mom, second, weight - step_rate * (update + decay_rate * weight))


def turn(block, cos_t, low_t, high_t):
    return block * cos_t + pltpu.roll(block, LANES - ROT // 2, 1) * low_t + pltpu.roll(block, ROT // 2, 1) * high_t

def assemble(upper_ref, upper_far_ref, lower_ref, lower_far_ref, rows_ref):
    half = lower_ref.shape[1]

    @pl.when(pl.program_id(0) == 0)
    def near():
        rows_ref[: 2 * half] = upper_ref[...].reshape(2 * half, -1)

    @pl.when(pl.program_id(0) == 1)
    def far():
        rows_ref[: 2 * half] = upper_far_ref[...].reshape(2 * half, -1)

    rows_ref[2 * half : 3 * half] = lower_ref[0]
    rows_ref[3 * half :] = lower_far_ref[0]


def forward_kernel(
    own,
    upper_ref,
    upper_far_ref,
    lower_ref,
    lower_far_ref,
    weight_ref,
    bias_ref,
    cos_ref,
    low_ref,
    high_ref,
    row_ref,
    column_ref,
    rows_ref,
    keep_ref,
    mix_ref,
    branch_ref,
):
    assemble(upper_ref, upper_far_ref, lower_ref, lower_far_ref, rows_ref)
    rows = rows_ref[...]
    length = rows.shape[0]
    cos_t, low_t, high_t = cos_ref[...], low_ref[...], high_ref[...]
    allowed = (row_ref[0, 0:1] <= column_ref[0, :, 0:1]) & (
        row_ref[0, 1:2] == column_ref[0, :, 1:2]
    )
    first_head = lax.broadcasted_iota(jnp.int32, (length, LANES), 1) < HD
    scale = HD**-0.5
    for part in range(3):
        cols = slice(part * own, (part + 1) * own)
        made = dot(rows, weight_ref[:, cols], 1, 0) + bias_ref[:, cols]
        for at in range(0, own, LANES):
            piece = made[:, at : at + LANES]
            if part < 2:
                piece = turn(piece, cos_t, low_t, high_t)
            keep_ref[:, part * own + at : part * own + at + LANES] = piece.astype(LOW)
    for at in range(0, own, LANES):
        q2 = keep_ref[:, at : at + LANES]
        k2 = keep_ref[:, own + at : own + at + LANES]
        v2 = keep_ref[:, 2 * own + at : 2 * own + at + LANES]
        outs = []
        for head in range(2):
            mine = first_head if head == 0 else ~first_head
            scored = dot(jnp.where(mine, q2, jnp.zeros_like(q2)), k2, 1, 1) * scale
            scored = jnp.where(allowed, scored, NEG_FILL)
            exponent = jnp.exp(scored - jnp.max(scored, axis=1, keepdims=True))
            total = jnp.sum(exponent, axis=1, keepdims=True)
            outs.append(dot((exponent * (1.0 / total)).astype(LOW), v2, 1, 0))
        mix_ref[:, at : at + LANES] = jnp.where(first_head, outs[0], outs[1]).astype(LOW)
    branch_ref[...] = dot(mix_ref[...], weight_ref[:, 3 * own :], 1, 1).astype(branch_ref.dtype)


def backward_kernel(
    own,
    upper_ref,
    upper_far_ref,
    lower_ref,
    lower_far_ref,
    weight_ref,
    keep_ref,
    cos_ref,
    low_ref,
    high_ref,
    row_ref,
    column_ref,
    rows_ref,
    grad_ref,
    normed_ref,
):
    assemble(upper_ref, upper_far_ref, lower_ref, lower_far_ref, rows_ref)
    length = rows_ref.shape[0]
    cos_t, low_t, high_t = cos_ref[...], -low_ref[...], -high_ref[...]
    allowed = (column_ref[0, :, 0:1] <= row_ref[0, 0:1]) & (
        row_ref[0, 1:2] == column_ref[0, :, 1:2]
    )
    first_head = lax.broadcasted_iota(jnp.int32, (length, LANES), 1) < HD
    scale = HD**-0.5
    d_mix = dot(rows_ref[...], weight_ref[:, 3 * own :], 1, 0).astype(LOW)
    for at in range(0, own, LANES):
        q2 = keep_ref[:, at : at + LANES]
        k2 = keep_ref[:, own + at : own + at + LANES]
        v2 = keep_ref[:, 2 * own + at : 2 * own + at + LANES]
        do2 = d_mix[:, at : at + LANES]
        dq, dk, dv = [], [], []
        for head in range(2):
            mine = first_head if head == 0 else ~first_head
            scored = dot(jnp.where(mine, k2, jnp.zeros_like(k2)), q2, 1, 1) * scale
            scored = jnp.where(allowed, scored, NEG_FILL)
            exponent = jnp.exp(scored - jnp.max(scored, axis=0, keepdims=True))
            weights = exponent * (1.0 / jnp.sum(exponent, axis=0, keepdims=True))
            d_weights = dot(jnp.where(mine, v2, jnp.zeros_like(v2)), do2, 1, 1)
            total = jnp.sum(weights * d_weights, axis=0, keepdims=True)
            d_scores = (weights * (d_weights - total)).astype(LOW)
            dv.append(dot(weights.astype(LOW), do2, 1, 0))
            dk.append(dot(d_scores, q2, 1, 0))
            dq.append(dot(d_scores, k2, 0, 0))
        for part, pair in enumerate((dq, dk, dv)):
            piece = jnp.where(first_head, pair[0], pair[1])
            if part < 2:
                piece = turn(piece * scale, cos_t, low_t, high_t)
            grad_ref[:, part * own + at : part * own + at + LANES] = piece.astype(LOW)
    normed_ref[...] = dot(grad_ref[...], weight_ref[:, : 3 * own], 1, 1).astype(normed_ref.dtype)


def both_halves(block, first_half):
    other = pltpu.roll(block, LANES // 2, 1)
    return jnp.where(first_half, block, other), jnp.where(first_half, other, block)


def mlp_kernel(
    main,
    upper_ref,
    upper_far_ref,
    lower_ref,
    lower_far_ref,
    weight_ref,
    rows_ref,
    gate_up_ref,
    hidden_ref,
):
    assemble(upper_ref, upper_far_ref, lower_ref, lower_far_ref, rows_ref)
    rows = rows_ref[...]
    for at in range(0, 2 * main + LANES, 2 * LANES):
        cols = slice(at, min(at + 2 * LANES, 2 * main + LANES))
        gate_up_ref[:, cols] = dot(rows, weight_ref[:, cols], 1, 0)
    for at in range(0, main, LANES):
        gate = gate_up_ref[:, at : at + LANES]
        up = gate_up_ref[:, main + at : main + at + LANES]
        hidden_ref[:, at : at + LANES] = (gate / (1.0 + jnp.exp(-gate)) * up).astype(LOW)
    last = gate_up_ref[:, 2 * main :]
    first_half = lax.broadcasted_iota(jnp.int32, last.shape, 1) < LANES // 2
    gate, up = both_halves(last, first_half)
    made = gate / (1.0 + jnp.exp(-gate)) * up
    hidden_ref[:, main:] = jnp.where(first_half, made, 0.0).astype(LOW)


def gate_up_back(gate, up, d_hidden):
    sigma = 1.0 / (1.0 + jnp.exp(-gate))
    d_gate = d_hidden * up * sigma * (1.0 + gate * (1.0 - sigma))
    return d_gate.astype(LOW), (d_hidden * (gate * sigma)).astype(LOW)


def mlp_back_kernel(main, rows_ref, down_ref, gate_up_ref, grad_ref):
    rows = rows_ref[...]
    for start in range(0, main + LANES, 2 * LANES):
        d_hidden = dot(rows, down_ref[:, start : start + 2 * LANES], 1, 0)
        for at in range(start, min(start + 2 * LANES, main), LANES):
            d_gate, d_up = gate_up_back(
                gate_up_ref[:, at : at + LANES],
                gate_up_ref[:, main + at : main + at + LANES],
                d_hidden[:, at - start : at - start + LANES],
            )
            grad_ref[:, at : at + LANES] = d_gate
            grad_ref[:, main + at : main + at + LANES] = d_up
    last = gate_up_ref[:, 2 * main :]
    first_half = lax.broadcasted_iota(jnp.int32, last.shape, 1) < LANES // 2
    gate, up = both_halves(last, first_half)
    d_hidden, _ = both_halves(d_hidden[:, main - start :], first_half)
    d_gate, d_up = gate_up_back(gate, up, d_hidden)
    grad_ref[:, 2 * main :] = jnp.where(first_half, d_gate, d_up)


def mlp_back_send_kernel(main, rows_ref, down_ref, weight_ref, gate_up_ref, grad_ref, sent_ref):
    mlp_back_kernel(main, rows_ref, down_ref, gate_up_ref, grad_ref)
    sent_ref[...] = dot(grad_ref[...], weight_ref[...], 1, 1).astype(LOW)


def add_kernel(
    left_ref, right_ref, got_ref, upper_sent_ref, lower_sent_ref, upper_ref, lower_ref
):
    total = dot(left_ref[...], right_ref[...], 1, 1) + got_ref[...].astype(F32)
    half = lower_ref.shape[1]

    @pl.when(pl.program_id(0) == 0)
    def near():
        upper_ref[...] = total[: 2 * half].reshape(2, half, -1)

    @pl.when(pl.program_id(0) == 1)
    def far():
        upper_sent_ref[...] = total[: 2 * half].reshape(2, half, -1).astype(LOW)

    lower_ref[0] = total[2 * half : 3 * half]
    lower_sent_ref[0] = total[3 * half :].astype(LOW)


def whole(shape):
    return pl.BlockSpec(shape, lambda i: (0,) * len(shape))


HELD = pl.BlockSpec(memory_space=pltpu.VMEM)


def sequences(length, width, first=0):
    return pl.BlockSpec((length, width), lambda i: (first + i, 0))


def piece_specs(pieces):
    upper, _, lower, _ = pieces
    moving = pl.BlockSpec((1, *lower.shape[1:]), lambda i: (i, 0, 0))
    return [whole(upper.shape), whole(upper.shape), moving, moving]


def info_specs(length, first):
    return [
        pl.BlockSpec((1, 2, length), lambda i: (first + i, 0, 0)),
        pl.BlockSpec((1, length, 2), lambda i: (first + i, 0, 0)),
    ]


def call(kernel, in_specs, out_specs, out_shape, flops, operands):
    return pl.pallas_call(
        kernel,
        grid=(2,),
        in_specs=in_specs,
        out_specs=out_specs,
        out_shape=[jax.ShapeDtypeStruct(*item) for item in out_shape],
        compiler_params=pltpu.CompilerParams(vmem_limit_bytes=KERNEL_BYTES),
        cost_estimate=pl.CostEstimate(flops=flops, bytes_accessed=0, transcendentals=0),
    )(*operands)


def collect(pieces, length):
    width = pieces[0].shape[2]
    return call(
        assemble,
        piece_specs(pieces),
        [sequences(length, width)],
        [((2 * length, width), LOW)],
        0,
        pieces,
    )[0]


def attend(pieces, weight, bias, tables, row_info, column_info, first, kind):
    length = row_info.shape[2]
    count = 2 * length
    width = weight.shape[0]
    own = weight.shape[1] // 4
    return call(
        functools.partial(forward_kernel, own),
        piece_specs(pieces)
        + [whole(weight.shape), whole(bias.shape)]
        + [whole(table.shape) for table in tables]
        + info_specs(length, first),
        [sequences(length, item) for item in (width, 3 * own, own, width)],
        [
            ((count, width), LOW),
            ((count, 3 * own), LOW),
            ((count, own), LOW),
            ((count, width), kind),
        ],
        2 * count * (width * 4 * own + 4 * length * own),
        (*pieces, weight, bias, *tables, row_info, column_info),
    )


def attend_back(pieces, weight, kept, tables, row_info, column_info, first, kind):
    length = row_info.shape[2]
    count = 2 * length
    width = weight.shape[0]
    own = weight.shape[1] // 4
    return call(
        functools.partial(backward_kernel, own),
        piece_specs(pieces)
        + [whole(weight.shape), sequences(length, 3 * own)]
        + [whole(table.shape) for table in tables]
        + info_specs(length, first),
        [sequences(length, item) for item in (width, 3 * own, width)],
        [((count, width), LOW), ((count, 3 * own), LOW), ((count, width), kind)],
        2 * count * (width * 4 * own + 10 * length * own),
        (*pieces, weight, kept, *tables, row_info, column_info),
    )


def mlp(pieces, weight, length):
    count = 2 * length
    width, both = weight.shape
    main = (both - LANES) // 2
    return call(
        functools.partial(mlp_kernel, main),
        piece_specs(pieces) + [whole(weight.shape)],
        [sequences(length, item) for item in (width, both, main + LANES)],
        [((count, width), LOW), ((count, both), F32), ((count, main + LANES), LOW)],
        2 * count * width * both,
        (*pieces, weight),
    )


def mlp_back(rows, down, gate_up, length, weight=None):
    count = 2 * length
    width = rows.shape[1]
    both = gate_up.shape[1]
    specs = [sequences(length, width), HELD, sequences(length, both)]
    operands = [rows, down, gate_up]
    kernel, widths = mlp_back_kernel, (both,)
    if weight is not None:
        specs.insert(2, HELD)
        operands.insert(2, weight)
        kernel, widths = mlp_back_send_kernel, (both, width)
    return call(
        functools.partial(kernel, (both - LANES) // 2),
        specs,
        [sequences(length, item) for item in widths],
        [((count, item), LOW) for item in widths],
        (2 * len(widths) - 1) * count * width * both,
        operands,
    )


def add_rows(left, right, got, length):
    half = length // 4
    width = right.shape[0]
    shape = (2, half, width)
    moving = pl.BlockSpec((1, half, width), lambda i: (i, 0, 0))
    return call(
        add_kernel,
        [sequences(length, left.shape[1]), HELD, sequences(length, width)],
        [whole(shape), moving, whole(shape), moving],
        [(shape, LOW), (shape, LOW), (shape, F32), (shape, F32)],
        4 * length * width * left.shape[1],
        (left, right, got),
    )


def grads_kernel(widths, *refs):
    out_ref = refs[-1]
    at = 0
    for k, width in enumerate(widths):
        left_here, left_away, right_here, right_away = refs[4 * k : 4 * k + 4]
        made = dot(left_here[...], right_here[...], 0, 0) + dot(
            left_away[...], right_away[...], 0, 0
        )
        out_ref[:, at : at + width] = made.astype(LOW)
        at += width


def grads(*parts):
    operands, specs, widths, flops = [], [], [], 0
    for lefts, rights in parts:
        count, width = rights[0].shape
        depth = lefts[0].shape[1]
        block = min(512, depth)
        for half, left in enumerate(lefts):
            row = half if left.shape[0] == 2 * count else 0
            specs.append(pl.BlockSpec((count, block), lambda i, row=row: (row, i)))
        specs += [whole(right.shape) for right in rights]
        operands += [*lefts, *rights]
        widths.append(width)
        flops += 4 * count * depth * width
    total = sum(widths)
    return pl.pallas_call(
        functools.partial(grads_kernel, tuple(widths)),
        grid=(depth // block,),
        in_specs=specs,
        out_specs=pl.BlockSpec((block, total), lambda i: (i, 0)),
        out_shape=jax.ShapeDtypeStruct((depth, total), LOW),
        compiler_params=pltpu.CompilerParams(vmem_limit_bytes=KERNEL_BYTES),
        cost_estimate=pl.CostEstimate(flops=flops, bytes_accessed=0, transcendentals=0),
    )(*operands)


def adamw_write(refs, index, gradient, step_rate, decay_rate):
    weight, first_mom, second, new_first, new_second, new_weight = refs
    made = adamw_update(
        weight[index], first_mom[index], second[index], gradient, step_rate, decay_rate
    )
    new_first[index], new_second[index], new_weight[index] = made


def piece_of(at_ref, near_ref, far_ref, quarter, cols):
    y_away = lax.rem(quarter // 2 + at_ref[0], 2)
    core_away = lax.rem(lax.rem(quarter, 2) + at_ref[1], 2)
    near = near_ref[core_away, :, cols]
    return jnp.where(y_away == 0, near, far_ref[core_away, :, cols]).astype(F32)


def attn_update_kernel(own, at_ref, near_ref, far_ref, *refs):
    quarter = pl.program_id(0)
    qkv, out = refs[0:3] + refs[6:9], refs[3:6] + refs[9:12]
    for part in range(3):
        cols = slice(part * own, (part + 1) * own)
        gradient = piece_of(at_ref, near_ref, far_ref, quarter, cols)
        adamw_write(qkv, part, gradient, RATE_MATRIX, DECAY_MATRIX)
    gradient = piece_of(at_ref, near_ref, far_ref, quarter, slice(3 * own, 4 * own))
    adamw_write(out, slice(None), gradient.T, RATE_OUT, DECAY_MATRIX)


def gate_up_update_kernel(main, at_ref, near_ref, far_ref, *refs):
    part = pl.program_id(0)
    rows = near_ref.shape[1]
    first_half = lax.broadcasted_iota(jnp.int32, (rows, LANES), 1) < LANES // 2
    tails = []
    for quarter in range(4):
        cols = pl.ds(pl.multiple_of(part * main, LANES), main)
        gradient = piece_of(at_ref, near_ref, far_ref, quarter, cols)
        index = (0, slice(None), slice(quarter * main, (quarter + 1) * main))
        adamw_write(refs, index, gradient, RATE_MATRIX, DECAY_MATRIX)
        last = piece_of(at_ref, near_ref, far_ref, quarter, slice(2 * main, 2 * main + LANES))
        tails.append((last, pltpu.roll(last, LANES // 2, 1)))
    for pair in range(2):
        (left, left_turned), (right, right_turned) = tails[2 * pair : 2 * pair + 2]
        left = jnp.where(part == 0, left, left_turned)
        right = jnp.where(part == 0, right_turned, right)
        at = 4 * main + pair * LANES
        index = (0, slice(None), slice(at, at + LANES))
        adamw_write(
            refs, index, jnp.where(first_half, left, right), RATE_MATRIX, DECAY_MATRIX
        )


def down_update_kernel(main, at_ref, near_ref, far_ref, *refs):
    for quarter in range(4):
        gradient = piece_of(at_ref, near_ref, far_ref, quarter, slice(0, main + LANES)).T
        for source, at, size in (
            (0, quarter * main, main),
            (main, 4 * main + quarter * (LANES // 2), LANES // 2),
        ):
            adamw_write(
                refs,
                slice(at, at + size),
                gradient[source : source + size],
                RATE_MATRIX,
                DECAY_MATRIX,
            )


def update(kernel, steps, specs, places, pieces, arrays):
    near, far = pieces
    return pl.pallas_call(
        kernel,
        grid_spec=pltpu.PrefetchScalarGridSpec(
            num_scalar_prefetch=1,
            grid=(steps,),
            in_specs=[pl.BlockSpec(near.shape, lambda i, at: (0, 0, 0))] * 2 + specs,
            out_specs=specs,
        ),
        out_shape=[jax.ShapeDtypeStruct(array.shape, F32) for array in arrays],
        compiler_params=pltpu.CompilerParams(vmem_limit_bytes=KERNEL_BYTES),
        cost_estimate=pl.CostEstimate(
            flops=0, bytes_accessed=24 * sum(array.size for array in arrays) // 3, transcendentals=0
        ),
    )(places, near, far, *arrays)


def gather_start(rows):
    half = rows.shape[0] // 2
    upper, lower = rows[:half], rows[half:]
    return upper, swap(upper, "tensor"), lower, swap(lower, "y")


def gather_near(upper, upper_x, lower, lower_y):
    upper_pair = jnp.stack([upper, upper_x])
    lower_pair = jnp.stack([lower, lower_y])
    return upper_pair, swap(upper_pair, "y"), lower_pair, swap(lower_pair, "tensor")


def gather_end(*flow):
    here = gather_near(*flow)
    return here, tuple(swap(piece, "core") for piece in here)


def gather_rows(rows):
    return gather_end(*gather_start(rows))


def reduce_start(here, away):
    away = swap(away, "core")
    total = (here.astype(F32) + away.astype(F32)).reshape(2, 2, 2, -1, here.shape[1])
    upper, lower = total[:, 0], total[:, 1]
    return upper[1].astype(LOW), lower[:, 1].astype(LOW), upper[0], lower[:, 0]


def reduce_first(upper_sent, lower_sent, upper, lower):
    return upper, swap(upper_sent, "y"), lower, swap(lower_sent, "tensor")


def reduce_second(upper, upper_got, lower, lower_got):
    upper = upper + upper_got.astype(F32)
    lower = lower + lower_got.astype(F32)
    return (
        upper[0],
        swap(upper[1].astype(LOW), "tensor"),
        lower[0],
        swap(lower[1].astype(LOW), "y"),
    )


def reduce_end(upper, upper_got, lower, lower_got):
    return jnp.concatenate(
        [upper + upper_got.astype(F32), lower + lower_got.astype(F32)], axis=0
    )


def reduce_rows(here, away):
    return reduce_end(*reduce_second(*reduce_first(*reduce_start(here, away))))


def tie(*items):
    return lax.optimization_barrier(items)


def spread_y(block, y_at):
    rows, _, width = block.shape
    block = block.reshape(rows, 2, 2, width)
    return in_order(pick(block, y_at, 1), swap(pick(block, 1 - y_at, 1), "y"), y_at)


def spread_core(block, core_at):
    other = swap(pick(block, 1 - core_at, 2), "core")
    block = in_order(pick(block, core_at, 2), other, core_at)
    return jnp.swapaxes(block, 0, 1).reshape(-1, block.shape[-1])


def gather_weights(block):
    return lax.all_gather(block, "z", axis=0, tiled=True)


def sum_weights(block):
    return lax.psum_scatter(block, "z", scatter_dimension=0, tiled=True)


def return_core(block, core_at):
    block = block.reshape(2, 2, -1, block.shape[1])
    return jnp.stack([pick(block, core_at, 1), swap(pick(block, 1 - core_at, 1), "core")])


def return_y(block, y_at):
    return pick(block, y_at, 1), swap(pick(block, 1 - y_at, 1), "y")


def return_weights(block, y_at, core_at):
    return return_y(return_core(block, core_at), y_at)


def sum_all(block, axes, size):
    step = 1
    while step < size:
        count = min(8, size // step)
        terms = [block] + [
            lax.ppermute(block, axes, [(i, i ^ (step * other)) for i in range(size)])
            for other in range(1, count)
        ]
        while len(terms) > 1:
            terms = [left + right for left, right in zip(terms[::2], terms[1::2])]
        block = terms[0]
        step *= count
    return block


def quarters(block):
    return block.reshape(block.shape[0], 4, -1)


def split_units(block, main):
    return quarters(block[:, : 4 * main]), quarters(block[:, 4 * main :])


def local(
    tokens,
    segment_ids,
    cotangent,
    w_qkv,
    m_qkv,
    v_qkv,
    w_out,
    m_out,
    v_out,
    w_gate_up,
    m_gate_up,
    v_gate_up,
    w_down,
    m_down,
    v_down,
    b_qkv,
    m_bias,
    v_bias,
    ln_params,
    m_norm,
    v_norm,
):
    share, model_width = tokens.shape
    length = segment_ids.shape[1]
    half_heads = b_qkv.shape[1]
    own_heads = half_heads // 4
    half_units = w_down.shape[0]
    main = half_units // 4 // LANES * LANES
    y_at = lax.axis_index("y")
    core_at = lax.axis_index("core")
    x_at = lax.axis_index("tensor")
    z_size = lax.axis_size("z")
    quarter_at = y_at * 2 + core_at

    w_qkv_low = w_qkv.astype(LOW)
    attn_block = jnp.concatenate(
        [quarters(w_qkv_low[k]) for k in range(3)] + [quarters(w_out.astype(LOW).T)], axis=2
    )
    gate_up_low = w_gate_up.astype(LOW)
    gate_main, gate_tail = split_units(gate_up_low[0], main)
    up_main, up_tail = split_units(gate_up_low[1], main)
    gate_up_block = jnp.concatenate([gate_main, up_main, gate_tail, up_tail], axis=2)
    down_main, down_tail = split_units(w_down.astype(LOW).T, main)
    down_block = jnp.concatenate([down_main, down_tail, jnp.zeros_like(down_tail)], axis=2)

    half = share // 2
    places = jnp.arange(half, dtype=jnp.int32)
    x_order = jnp.stack([x_at, 1 - x_at])
    positions = (
        jnp.arange(2, dtype=jnp.int32)[:, None, None] * half
        + x_order[None, :, None] * share
        + places[None, None, :]
    ).reshape(length)
    tables = angle_tables(positions)
    ids = segment_ids[0].reshape(2, 2, half)
    ids = jnp.swapaxes(jnp.where(x_at == 0, ids, ids[::-1]), 0, 1).reshape(length)
    bias = lax.dynamic_slice_in_dim(b_qkv, quarter_at * own_heads, own_heads, 1).reshape(1, -1)

    inputs_f = tokens.astype(F32)
    hat_a, scale_a = norm_stats(inputs_f)
    a_low = (hat_a * ln_params[0] + ln_params[1]).astype(LOW)
    attn_block = spread_core(spread_y(attn_block, y_at), core_at)
    attn_block, a_low, ids, gate_up_block = tie(attn_block, a_low, ids, gate_up_block)
    attn_full = gather_weights(attn_block)
    gate_up_block = spread_y(gate_up_block, y_at)
    ids = jnp.stack([ids, swap(ids, "y")])
    flow, ids, gate_up_block = tie(gather_start(a_low), ids, gate_up_block)
    gate_up_block = spread_core(gate_up_block, core_at)
    ids = jnp.stack([ids, swap(ids, "core")]).reshape(4, length)
    row_info = jnp.stack([jnp.broadcast_to(positions, ids.shape), ids], axis=1)
    column_info = jnp.swapaxes(row_info, 1, 2)
    a_here, a_away = gather_end(*flow)
    a_here, gate_up_block, row_info, column_info, cot_low, down_block = tie(
        a_here, gate_up_block, row_info, column_info, cotangent, down_block
    )
    gate_up_full = gather_weights(gate_up_block)
    flow, down_block, a_here, a_away = tie(
        gather_start(cot_low), spread_y(down_block, y_at), a_here, a_away
    )
    down_block = spread_core(down_block, core_at)
    cot_here = gather_near(*flow)
    seq_info = (tables, row_info, column_info)
    a_rows_away, kept_away, mix_away, branch_away = attend(
        a_away, attn_full, bias, *seq_info, 2, LOW
    )
    down_full = gather_weights(down_block)
    a_rows_here, kept_here, mix_here, branch_here = attend(
        a_here, attn_full, bias, *seq_info, 0, F32
    )
    cot_here, branch_here = tie(cot_here, branch_here)
    flow = reduce_first(*reduce_start(branch_here, branch_away))
    cot_away = tuple(swap(piece, "core") for piece in cot_here)
    flow, cot_here, cot_away = tie(flow, collect(cot_here, length), collect(cot_away, length))
    middle = inputs_f + reduce_end(*reduce_second(*flow))
    hat_c, scale_c = norm_stats(middle)
    c_here, c_away = gather_rows((hat_c * ln_params[2] + ln_params[3]).astype(LOW))
    c_rows_here, gate_up_here, hidden_here = mlp(c_here, gate_up_full, length)
    c_rows_away, gate_up_away, hidden_away = mlp(c_away, gate_up_full, length)
    grad_down = grads(((cot_here, cot_away), (hidden_here, hidden_away)))
    cot_here, cot_away, grad_down = tie(cot_here, cot_away, grad_down)
    down_sum = sum_weights(grad_down)
    mlp_away, normed_away = mlp_back(cot_away, down_full, gate_up_away, length, gate_up_full)
    (mlp_here,) = mlp_back(cot_here, down_full, gate_up_here, length)
    flow = add_rows(mlp_here, gate_up_full, swap(normed_away, "core"), length)
    flow, mlp_here, mlp_away = tie(flow, mlp_here, mlp_away)
    grad_gate_up = grads(((c_rows_here, c_rows_away), (mlp_here, mlp_away)))
    flow, grad_gate_up, hidden_here, hidden_away = tie(
        reduce_first(*flow), grad_gate_up, hidden_here, hidden_away
    )
    gate_up_sum = sum_weights(grad_gate_up)
    result_away = dot(hidden_away, down_full, 1, 1).astype(LOW)
    flow, result_away, hidden_here = tie(reduce_second(*flow), result_away, hidden_here)
    d_normed_c = reduce_end(*flow)

    d_middle_n, d_gain_c, d_shift_c = norm_back(hat_c, scale_c, ln_params[2], d_normed_c)
    d_middle = cotangent.astype(F32) + d_middle_n
    result = add_rows(hidden_here, down_full, swap(result_away, "core"), length)
    flow, result = tie(gather_start(d_middle.astype(LOW)), result)
    branch_here, branch_away = gather_end(*flow)
    branch_here, result = tie(branch_here, result)
    result = reduce_first(*result)
    b_rows_here, back_here, normed_here = attend_back(
        branch_here, attn_full, kept_here, *seq_info, 0, F32
    )
    b_rows_away, back_away, normed_away = attend_back(
        branch_away, attn_full, kept_away, *seq_info, 2, LOW
    )
    down_sum = return_weights(down_sum, y_at, core_at)
    result, back_away, down_sum = tie(result, back_away, down_sum)
    grad_attn = grads(
        ((a_rows_here, a_rows_away), (back_here, back_away)),
        ((b_rows_here, b_rows_away), (mix_here, mix_away)),
    )
    grad_attn, normed_here, normed_away, back_here, back_away, result, down_sum = tie(
        grad_attn, normed_here, normed_away, back_here, back_away, result, down_sum
    )
    attn_sum = sum_weights(grad_attn)
    flow, gate_up_sum, down_sum = tie(
        reduce_first(*reduce_start(normed_here, normed_away)),
        return_core(gate_up_sum, core_at),
        down_sum,
    )
    flow, result, down_sum = tie(reduce_second(*flow), result, down_sum)
    d_normed_a = reduce_end(*flow)
    gate_up_sum = return_y(gate_up_sum, y_at)
    result = reduce_second(*result)
    d_input_n, d_gain_a, d_shift_a = norm_back(hat_a, scale_a, ln_params[0], d_normed_a)
    input_grad = d_middle + d_input_n

    bias_part = jnp.sum(back_here.astype(F32), axis=0) + jnp.sum(back_away.astype(F32), axis=0)
    bias_full = lax.dynamic_update_slice_in_dim(
        jnp.zeros((3, model_width), F32),
        bias_part.reshape(3, own_heads),
        x_at * half_heads + quarter_at * own_heads,
        1,
    )
    small = jnp.concatenate(
        [jnp.stack([d_gain_a, d_shift_a, d_gain_c, d_shift_c]), bias_full], axis=0
    )
    small = sum_all(small, "z", z_size)
    small, gate_up_sum, result = tie(small, gate_up_sum, result)
    small = sum_all(small, ("y", "core", "tensor"), 8)
    output = (middle + reduce_end(*result)).astype(LOW)
    norm_grad = small[:4]
    bias_grad = lax.dynamic_slice_in_dim(small[4:], x_at * half_heads, half_heads, 1)

    m_bias_new, v_bias_new, b_qkv_new = adamw_update(
        b_qkv, m_bias, v_bias, bias_grad, RATE_SMALL, 0.0
    )
    m_norm_new, v_norm_new, ln_params_new = adamw_update(
        ln_params, m_norm, v_norm, norm_grad, RATE_SMALL, 0.0
    )
    bias_new = (m_bias_new, v_bias_new, b_qkv_new)
    norm_new = (m_norm_new, v_norm_new, ln_params_new)
    attn_sum, output, input_grad, bias_new, norm_new, gate_up_sum, down_sum = tie(
        attn_sum, output, input_grad, bias_new, norm_new, gate_up_sum, down_sum
    )
    places = jnp.stack([y_at, core_at]).astype(jnp.int32)
    rows = w_qkv.shape[1]
    stacked = pl.BlockSpec((1, *w_gate_up.shape[1:]), lambda i, at: (i, 0, 0))
    gate_up_new = update(
        functools.partial(gate_up_update_kernel, main),
        2,
        [stacked] * 3,
        places,
        gate_up_sum,
        (w_gate_up, m_gate_up, v_gate_up),
    )
    flat = pl.BlockSpec(w_down.shape, lambda i, at: (0, 0))
    down_new = update(
        functools.partial(down_update_kernel, main),
        1,
        [flat] * 3,
        places,
        down_sum,
        (w_down, m_down, v_down),
    )
    qkv = pl.BlockSpec((3, rows, own_heads), lambda i, at: (0, 0, i))
    out = pl.BlockSpec((own_heads, rows), lambda i, at: (i, 0))
    attn_new = update(
        functools.partial(attn_update_kernel, own_heads),
        4,
        [qkv] * 3 + [out] * 3,
        places,
        return_weights(attn_sum, y_at, core_at),
        (w_qkv, m_qkv, v_qkv, w_out, m_out, v_out),
    )
    return (output, input_grad, *attn_new, *gate_up_new, *down_new, *bias_new, *norm_new)


def solution(mesh):
    owners = mesh.shape["dp"]
    pair = mesh.shape["tensor"]
    cut = Mesh(mesh.devices.reshape(owners // 4, 2, 2, pair), ("z", "y", "core", "tensor"))
    dp = ("z", "y", "core")
    rows = P((*dp, "tensor"), None)
    stacked = P(None, dp, "tensor")
    flat = P("tensor", dp)
    bias = P(None, "tensor")
    in_specs = (
        (rows, P(dp, None), rows)
        + (stacked,) * 3
        + (flat,) * 3
        + (stacked,) * 3
        + (flat,) * 3
        + (bias,) * 3
        + (P(),) * 3
    )
    out_specs = (
        (rows, rows)
        + (stacked,) * 3
        + (flat,) * 3
        + (stacked,) * 3
        + (flat,) * 3
        + (bias,) * 3
        + (P(),) * 3
    )
    return jax.shard_map(local, mesh=cut, in_specs=in_specs, out_specs=out_specs, check_vma=False)
```

```python
import functools

import jax
import jax.numpy as jnp
from jax import lax
from jax.experimental import pallas as pl
from jax.experimental.pallas import tpu as pltpu
from jax.sharding import Mesh
from jax.sharding import PartitionSpec as P

HD = 64
ROT = 16
STEP_COUNT = 10

EPS = 1e-05
NEG_FILL = -1000000000.0
BETA_ONE = 0.9
BETA_TWO = 0.95
ADAM_EPS = 1e-08
RATE_MATRIX = 0.01
RATE_OUT = 0.05
RATE_SMALL = 0.25
DECAY_MATRIX = 0.1

LOW = jnp.bfloat16
F32 = jnp.float32
LANES = 128
KERNEL_BYTES = 42 * 2**20


def dot(left, right, left_dim, right_dim):
    return lax.dot_general(
        left, right, (((left_dim,), (right_dim,)), ((), ())), preferred_element_type=F32
    )


def swap(block, axis):
    return lax.ppermute(block, axis, [(0, 1), (1, 0)])


def pick(block, index, dim):
    return lax.dynamic_index_in_dim(block, index, dim, keepdims=False)


def in_order(own, other, index):
    first = index == 0
    return jnp.stack([jnp.where(first, own, other), jnp.where(first, other, own)])


def norm_stats(row_data):
    average = jnp.mean(row_data, axis=-1, keepdims=True)
    centered = row_data - average
    variance = jnp.mean(centered * centered, axis=-1, keepdims=True)
    scale = lax.rsqrt(variance + EPS)
    return centered * scale, scale


def norm_back(hat, scale, gain_vec, grad):
    scaled = grad * gain_vec
    row_grad = (
        scaled
        - jnp.mean(scaled, axis=-1, keepdims=True)
        - hat * jnp.mean(scaled * hat, axis=-1, keepdims=True)
    ) * scale
    return row_grad, jnp.sum(grad * hat, axis=0), jnp.sum(grad, axis=0)


def angle_tables(positions):
    half_rot = ROT // 2
    frequency = 10000.0 ** (-2.0 * jnp.arange(half_rot, dtype=jnp.int32).astype(F32) / ROT)
    angle_table = positions.astype(F32)[:, None] * frequency[None, :]
    cos_part, sin_part = jnp.cos(angle_table), jnp.sin(angle_table)
    rest = jnp.zeros((positions.shape[0], HD - ROT), F32)
    none = jnp.zeros_like(sin_part)

    def table(*parts):
        return jnp.tile(jnp.concatenate(parts, axis=1), (1, LANES // HD))

    return (
        table(cos_part, cos_part, rest + 1.0),
        table(-sin_part, none, rest),
        table(none, sin_part, rest),
    )


def adamw_update(weight, first_mom, second, gradient, step_rate, decay_rate):
    first_mom = BETA_ONE * first_mom + (1.0 - BETA_ONE) * gradient
    second = BETA_TWO * second + (1.0 - BETA_TWO) * gradient * gradient
    fix_first = 1.0 - BETA_ONE**STEP_COUNT
    fix_second = 1.0 - BETA_TWO**STEP_COUNT
    update = first_mom / fix_first / (jnp.sqrt(second / fix_second) + ADAM_EPS)
    return (first_mom, second, weight - step_rate * (update + decay_rate * weight))


def turn(block, cos_t, low_t, high_t):
    return block * cos_t + pltpu.roll(block, LANES - ROT // 2, 1) * low_t + pltpu.roll(block, ROT // 2, 1) * high_t

def assemble(upper_ref, upper_far_ref, lower_ref, lower_far_ref, rows_ref):
    half = lower_ref.shape[1]

    @pl.when(pl.program_id(0) == 0)
    def near():
        rows_ref[: 2 * half] = upper_ref[...].reshape(2 * half, -1)

    @pl.when(pl.program_id(0) == 1)
    def far():
        rows_ref[: 2 * half] = upper_far_ref[...].reshape(2 * half, -1)

    rows_ref[2 * half : 3 * half] = lower_ref[0]
    rows_ref[3 * half :] = lower_far_ref[0]


def forward_kernel(
    own,
    upper_ref,
    upper_far_ref,
    lower_ref,
    lower_far_ref,
    weight_ref,
    bias_ref,
    cos_ref,
    low_ref,
    high_ref,
    row_ref,
    column_ref,
    rows_ref,
    keep_ref,
    mix_ref,
    branch_ref,
):
    assemble(upper_ref, upper_far_ref, lower_ref, lower_far_ref, rows_ref)
    rows = rows_ref[...]
    length = rows.shape[0]
    cos_t, low_t, high_t = cos_ref[...], low_ref[...], high_ref[...]
    allowed = (row_ref[0, 0:1] <= column_ref[0, :, 0:1]) & (
        row_ref[0, 1:2] == column_ref[0, :, 1:2]
    )
    first_head = lax.broadcasted_iota(jnp.int32, (length, LANES), 1) < HD
    scale = HD**-0.5
    for part in range(3):
        cols = slice(part * own, (part + 1) * own)
        made = dot(rows, weight_ref[:, cols], 1, 0) + bias_ref[:, cols]
        for at in range(0, own, LANES):
            piece = made[:, at : at + LANES]
            if part < 2:
                piece = turn(piece, cos_t, low_t, high_t)
            keep_ref[:, part * own + at : part * own + at + LANES] = piece.astype(LOW)
    for at in range(0, own, LANES):
        q2 = keep_ref[:, at : at + LANES]
        k2 = keep_ref[:, own + at : own + at + LANES]
        v2 = keep_ref[:, 2 * own + at : 2 * own + at + LANES]
        outs = []
        for head in range(2):
            mine = first_head if head == 0 else ~first_head
            scored = dot(jnp.where(mine, q2, jnp.zeros_like(q2)), k2, 1, 1) * scale
            scored = jnp.where(allowed, scored, NEG_FILL)
            exponent = jnp.exp(scored - jnp.max(scored, axis=1, keepdims=True))
            total = jnp.sum(exponent, axis=1, keepdims=True)
            outs.append(dot((exponent * (1.0 / total)).astype(LOW), v2, 1, 0))
        mix_ref[:, at : at + LANES] = jnp.where(first_head, outs[0], outs[1]).astype(LOW)
    branch_ref[...] = dot(mix_ref[...], weight_ref[:, 3 * own :], 1, 1).astype(branch_ref.dtype)


def backward_kernel(
    own,
    upper_ref,
    upper_far_ref,
    lower_ref,
    lower_far_ref,
    weight_ref,
    keep_ref,
    cos_ref,
    low_ref,
    high_ref,
    row_ref,
    column_ref,
    rows_ref,
    grad_ref,
    normed_ref,
):
    assemble(upper_ref, upper_far_ref, lower_ref, lower_far_ref, rows_ref)
    length = rows_ref.shape[0]
    cos_t, low_t, high_t = cos_ref[...], -low_ref[...], -high_ref[...]
    allowed = (column_ref[0, :, 0:1] <= row_ref[0, 0:1]) & (
        row_ref[0, 1:2] == column_ref[0, :, 1:2]
    )
    first_head = lax.broadcasted_iota(jnp.int32, (length, LANES), 1) < HD
    scale = HD**-0.5
    d_mix = dot(rows_ref[...], weight_ref[:, 3 * own :], 1, 0).astype(LOW)
    for at in range(0, own, LANES):
        q2 = keep_ref[:, at : at + LANES]
        k2 = keep_ref[:, own + at : own + at + LANES]
        v2 = keep_ref[:, 2 * own + at : 2 * own + at + LANES]
        do2 = d_mix[:, at : at + LANES]
        dq, dk, dv = [], [], []
        for head in range(2):
            mine = first_head if head == 0 else ~first_head
            scored = dot(jnp.where(mine, k2, jnp.zeros_like(k2)), q2, 1, 1) * scale
            scored = jnp.where(allowed, scored, NEG_FILL)
            exponent = jnp.exp(scored - jnp.max(scored, axis=0, keepdims=True))
            weights = exponent * (1.0 / jnp.sum(exponent, axis=0, keepdims=True))
            d_weights = dot(jnp.where(mine, v2, jnp.zeros_like(v2)), do2, 1, 1)
            total = jnp.sum(weights * d_weights, axis=0, keepdims=True)
            d_scores = (weights * (d_weights - total)).astype(LOW)
            dv.append(dot(weights.astype(LOW), do2, 1, 0))
            dk.append(dot(d_scores, q2, 1, 0))
            dq.append(dot(d_scores, k2, 0, 0))
        for part, pair in enumerate((dq, dk, dv)):
            piece = jnp.where(first_head, pair[0], pair[1])
            if part < 2:
                piece = turn(piece * scale, cos_t, low_t, high_t)
            grad_ref[:, part * own + at : part * own + at + LANES] = piece.astype(LOW)
    normed_ref[...] = dot(grad_ref[...], weight_ref[:, : 3 * own], 1, 1).astype(normed_ref.dtype)


def both_halves(block, first_half):
    other = pltpu.roll(block, LANES // 2, 1)
    return jnp.where(first_half, block, other), jnp.where(first_half, other, block)


def mlp_kernel(
    main,
    upper_ref,
    upper_far_ref,
    lower_ref,
    lower_far_ref,
    weight_ref,
    rows_ref,
    gate_up_ref,
    hidden_ref,
):
    assemble(upper_ref, upper_far_ref, lower_ref, lower_far_ref, rows_ref)
    rows = rows_ref[...]
    for at in range(0, 2 * main + LANES, 2 * LANES):
        cols = slice(at, min(at + 2 * LANES, 2 * main + LANES))
        gate_up_ref[:, cols] = dot(rows, weight_ref[:, cols], 1, 0)
    for at in range(0, main, LANES):
        gate = gate_up_ref[:, at : at + LANES]
        up = gate_up_ref[:, main + at : main + at + LANES]
        hidden_ref[:, at : at + LANES] = (gate / (1.0 + jnp.exp(-gate)) * up).astype(LOW)
    last = gate_up_ref[:, 2 * main :]
    first_half = lax.broadcasted_iota(jnp.int32, last.shape, 1) < LANES // 2
    gate, up = both_halves(last, first_half)
    made = gate / (1.0 + jnp.exp(-gate)) * up
    hidden_ref[:, main:] = jnp.where(first_half, made, 0.0).astype(LOW)


def gate_up_back(gate, up, d_hidden):
    sigma = 1.0 / (1.0 + jnp.exp(-gate))
    d_gate = d_hidden * up * sigma * (1.0 + gate * (1.0 - sigma))
    return d_gate.astype(LOW), (d_hidden * (gate * sigma)).astype(LOW)


def mlp_back_kernel(main, rows_ref, down_ref, gate_up_ref, grad_ref):
    rows = rows_ref[...]
    for start in range(0, main + LANES, 2 * LANES):
        d_hidden = dot(rows, down_ref[:, start : start + 2 * LANES], 1, 0)
        for at in range(start, min(start + 2 * LANES, main), LANES):
            d_gate, d_up = gate_up_back(
                gate_up_ref[:, at : at + LANES],
                gate_up_ref[:, main + at : main + at + LANES],
                d_hidden[:, at - start : at - start + LANES],
            )
            grad_ref[:, at : at + LANES] = d_gate
            grad_ref[:, main + at : main + at + LANES] = d_up
    last = gate_up_ref[:, 2 * main :]
    first_half = lax.broadcasted_iota(jnp.int32, last.shape, 1) < LANES // 2
    gate, up = both_halves(last, first_half)
    d_hidden, _ = both_halves(d_hidden[:, main - start :], first_half)
    d_gate, d_up = gate_up_back(gate, up, d_hidden)
    grad_ref[:, 2 * main :] = jnp.where(first_half, d_gate, d_up)


def mlp_back_send_kernel(main, rows_ref, down_ref, weight_ref, gate_up_ref, grad_ref, sent_ref):
    mlp_back_kernel(main, rows_ref, down_ref, gate_up_ref, grad_ref)
    sent_ref[...] = dot(grad_ref[...], weight_ref[...], 1, 1).astype(LOW)


def add_kernel(
    left_ref, right_ref, got_ref, upper_sent_ref, lower_sent_ref, upper_ref, lower_ref
):
    total = dot(left_ref[...], right_ref[...], 1, 1) + got_ref[...].astype(F32)
    half = lower_ref.shape[1]

    @pl.when(pl.program_id(0) == 0)
    def near():
        upper_ref[...] = total[: 2 * half].reshape(2, half, -1)

    @pl.when(pl.program_id(0) == 1)
    def far():
        upper_sent_ref[...] = total[: 2 * half].reshape(2, half, -1).astype(LOW)

    lower_ref[0] = total[2 * half : 3 * half]
    lower_sent_ref[0] = total[3 * half :].astype(LOW)


def whole(shape):
    return pl.BlockSpec(shape, lambda i: (0,) * len(shape))


HELD = pl.BlockSpec(memory_space=pltpu.VMEM)


def sequences(length, width, first=0):
    return pl.BlockSpec((length, width), lambda i: (first + i, 0))


def piece_specs(pieces):
    upper, _, lower, _ = pieces
    moving = pl.BlockSpec((1, *lower.shape[1:]), lambda i: (i, 0, 0))
    return [whole(upper.shape), whole(upper.shape), moving, moving]


def info_specs(length, first):
    return [
        pl.BlockSpec((1, 2, length), lambda i: (first + i, 0, 0)),
        pl.BlockSpec((1, length, 2), lambda i: (first + i, 0, 0)),
    ]


def call(kernel, in_specs, out_specs, out_shape, flops, operands):
    return pl.pallas_call(
        kernel,
        grid=(2,),
        in_specs=in_specs,
        out_specs=out_specs,
        out_shape=[jax.ShapeDtypeStruct(*item) for item in out_shape],
        compiler_params=pltpu.CompilerParams(vmem_limit_bytes=KERNEL_BYTES),
        cost_estimate=pl.CostEstimate(flops=flops, bytes_accessed=0, transcendentals=0),
    )(*operands)


def collect(pieces, length):
    width = pieces[0].shape[2]
    return call(
        assemble,
        piece_specs(pieces),
        [sequences(length, width)],
        [((2 * length, width), LOW)],
        0,
        pieces,
    )[0]


def attend(pieces, weight, bias, tables, row_info, column_info, first, kind):
    length = row_info.shape[2]
    count = 2 * length
    width = weight.shape[0]
    own = weight.shape[1] // 4
    return call(
        functools.partial(forward_kernel, own),
        piece_specs(pieces)
        + [whole(weight.shape), whole(bias.shape)]
        + [whole(table.shape) for table in tables]
        + info_specs(length, first),
        [sequences(length, item) for item in (width, 3 * own, own, width)],
        [
            ((count, width), LOW),
            ((count, 3 * own), LOW),
            ((count, own), LOW),
            ((count, width), kind),
        ],
        2 * count * (width * 4 * own + 4 * length * own),
        (*pieces, weight, bias, *tables, row_info, column_info),
    )


def attend_back(pieces, weight, kept, tables, row_info, column_info, first, kind):
    length = row_info.shape[2]
    count = 2 * length
    width = weight.shape[0]
    own = weight.shape[1] // 4
    return call(
        functools.partial(backward_kernel, own),
        piece_specs(pieces)
        + [whole(weight.shape), sequences(length, 3 * own)]
        + [whole(table.shape) for table in tables]
        + info_specs(length, first),
        [sequences(length, item) for item in (width, 3 * own, width)],
        [((count, width), LOW), ((count, 3 * own), LOW), ((count, width), kind)],
        2 * count * (width * 4 * own + 10 * length * own),
        (*pieces, weight, kept, *tables, row_info, column_info),
    )


def mlp(pieces, weight, length):
    count = 2 * length
    width, both = weight.shape
    main = (both - LANES) // 2
    return call(
        functools.partial(mlp_kernel, main),
        piece_specs(pieces) + [whole(weight.shape)],
        [sequences(length, item) for item in (width, both, main + LANES)],
        [((count, width), LOW), ((count, both), F32), ((count, main + LANES), LOW)],
        2 * count * width * both,
        (*pieces, weight),
    )


def mlp_back(rows, down, gate_up, length, weight=None):
    count = 2 * length
    width = rows.shape[1]
    both = gate_up.shape[1]
    specs = [sequences(length, width), HELD, sequences(length, both)]
    operands = [rows, down, gate_up]
    kernel, widths = mlp_back_kernel, (both,)
    if weight is not None:
        specs.insert(2, HELD)
        operands.insert(2, weight)
        kernel, widths = mlp_back_send_kernel, (both, width)
    return call(
        functools.partial(kernel, (both - LANES) // 2),
        specs,
        [sequences(length, item) for item in widths],
        [((count, item), LOW) for item in widths],
        (2 * len(widths) - 1) * count * width * both,
        operands,
    )


def add_rows(left, right, got, length):
    half = length // 4
    width = right.shape[0]
    shape = (2, half, width)
    moving = pl.BlockSpec((1, half, width), lambda i: (i, 0, 0))
    return call(
        add_kernel,
        [sequences(length, left.shape[1]), HELD, sequences(length, width)],
        [whole(shape), moving, whole(shape), moving],
        [(shape, LOW), (shape, LOW), (shape, F32), (shape, F32)],
        4 * length * width * left.shape[1],
        (left, right, got),
    )


def grads_kernel(widths, *refs):
    out_ref = refs[-1]
    at = 0
    for k, width in enumerate(widths):
        left_here, left_away, right_here, right_away = refs[4 * k : 4 * k + 4]
        made = dot(left_here[...], right_here[...], 0, 0) + dot(
            left_away[...], right_away[...], 0, 0
        )
        out_ref[:, at : at + width] = made.astype(LOW)
        at += width


def grads(*parts):
    operands, specs, widths, flops = [], [], [], 0
    for lefts, rights in parts:
        count, width = rights[0].shape
        depth = lefts[0].shape[1]
        block = min(512, depth)
        for half, left in enumerate(lefts):
            row = half if left.shape[0] == 2 * count else 0
            specs.append(pl.BlockSpec((count, block), lambda i, row=row: (row, i)))
        specs += [whole(right.shape) for right in rights]
        operands += [*lefts, *rights]
        widths.append(width)
        flops += 4 * count * depth * width
    total = sum(widths)
    return pl.pallas_call(
        functools.partial(grads_kernel, tuple(widths)),
        grid=(depth // block,),
        in_specs=specs,
        out_specs=pl.BlockSpec((block, total), lambda i: (i, 0)),
        out_shape=jax.ShapeDtypeStruct((depth, total), LOW),
        compiler_params=pltpu.CompilerParams(vmem_limit_bytes=KERNEL_BYTES),
        cost_estimate=pl.CostEstimate(flops=flops, bytes_accessed=0, transcendentals=0),
    )(*operands)


def adamw_write(refs, index, gradient, step_rate, decay_rate):
    weight, first_mom, second, new_first, new_second, new_weight = refs
    made = adamw_update(
        weight[index], first_mom[index], second[index], gradient, step_rate, decay_rate
    )
    new_first[index], new_second[index], new_weight[index] = made


def piece_of(at_ref, near_ref, far_ref, quarter, cols):
    y_away = lax.rem(quarter // 2 + at_ref[0], 2)
    core_away = lax.rem(lax.rem(quarter, 2) + at_ref[1], 2)
    near = near_ref[core_away, :, cols]
    return jnp.where(y_away == 0, near, far_ref[core_away, :, cols]).astype(F32)


def attn_update_kernel(own, at_ref, near_ref, far_ref, *refs):
    quarter = pl.program_id(0)
    qkv, out = refs[0:3] + refs[6:9], refs[3:6] + refs[9:12]
    for part in range(3):
        cols = slice(part * own, (part + 1) * own)
        gradient = piece_of(at_ref, near_ref, far_ref, quarter, cols)
        adamw_write(qkv, part, gradient, RATE_MATRIX, DECAY_MATRIX)
    gradient = piece_of(at_ref, near_ref, far_ref, quarter, slice(3 * own, 4 * own))
    adamw_write(out, slice(None), gradient.T, RATE_OUT, DECAY_MATRIX)


def gate_up_update_kernel(main, at_ref, near_ref, far_ref, *refs):
    part = pl.program_id(0)
    rows = near_ref.shape[1]
    first_half = lax.broadcasted_iota(jnp.int32, (rows, LANES), 1) < LANES // 2
    tails = []
    for quarter in range(4):
        cols = pl.ds(pl.multiple_of(part * main, LANES), main)
        gradient = piece_of(at_ref, near_ref, far_ref, quarter, cols)
        index = (0, slice(None), slice(quarter * main, (quarter + 1) * main))
        adamw_write(refs, index, gradient, RATE_MATRIX, DECAY_MATRIX)
        last = piece_of(at_ref, near_ref, far_ref, quarter, slice(2 * main, 2 * main + LANES))
        tails.append((last, pltpu.roll(last, LANES // 2, 1)))
    for pair in range(2):
        (left, left_turned), (right, right_turned) = tails[2 * pair : 2 * pair + 2]
        left = jnp.where(part == 0, left, left_turned)
        right = jnp.where(part == 0, right_turned, right)
        at = 4 * main + pair * LANES
        index = (0, slice(None), slice(at, at + LANES))
        adamw_write(
            refs, index, jnp.where(first_half, left, right), RATE_MATRIX, DECAY_MATRIX
        )


def down_update_kernel(main, at_ref, near_ref, far_ref, *refs):
    for quarter in range(4):
        gradient = piece_of(at_ref, near_ref, far_ref, quarter, slice(0, main + LANES)).T
        for source, at, size in (
            (0, quarter * main, main),
            (main, 4 * main + quarter * (LANES // 2), LANES // 2),
        ):
            adamw_write(
                refs,
                slice(at, at + size),
                gradient[source : source + size],
                RATE_MATRIX,
                DECAY_MATRIX,
            )


def update(kernel, steps, specs, places, pieces, arrays):
    near, far = pieces
    return pl.pallas_call(
        kernel,
        grid_spec=pltpu.PrefetchScalarGridSpec(
            num_scalar_prefetch=1,
            grid=(steps,),
            in_specs=[pl.BlockSpec(near.shape, lambda i, at: (0, 0, 0))] * 2 + specs,
            out_specs=specs,
        ),
        out_shape=[jax.ShapeDtypeStruct(array.shape, F32) for array in arrays],
        compiler_params=pltpu.CompilerParams(vmem_limit_bytes=KERNEL_BYTES),
        cost_estimate=pl.CostEstimate(
            flops=0, bytes_accessed=24 * sum(array.size for array in arrays) // 3, transcendentals=0
        ),
    )(places, near, far, *arrays)


def gather_start(rows):
    half = rows.shape[0] // 2
    upper, lower = rows[:half], rows[half:]
    return upper, swap(upper, "tensor"), lower, swap(lower, "y")


def gather_near(upper, upper_x, lower, lower_y):
    upper_pair = jnp.stack([upper, upper_x])
    lower_pair = jnp.stack([lower, lower_y])
    return upper_pair, swap(upper_pair, "y"), lower_pair, swap(lower_pair, "tensor")


def gather_end(*flow):
    here = gather_near(*flow)
    return here, tuple(swap(piece, "core") for piece in here)


def gather_rows(rows):
    return gather_end(*gather_start(rows))


def reduce_start(here, away):
    away = swap(away, "core")
    total = (here.astype(F32) + away.astype(F32)).reshape(2, 2, 2, -1, here.shape[1])
    upper, lower = total[:, 0], total[:, 1]
    return upper[1].astype(LOW), lower[:, 1].astype(LOW), upper[0], lower[:, 0]


def reduce_first(upper_sent, lower_sent, upper, lower):
    return upper, swap(upper_sent, "y"), lower, swap(lower_sent, "tensor")


def reduce_second(upper, upper_got, lower, lower_got):
    upper = upper + upper_got.astype(F32)
    lower = lower + lower_got.astype(F32)
    return (
        upper[0],
        swap(upper[1].astype(LOW), "tensor"),
        lower[0],
        swap(lower[1].astype(LOW), "y"),
    )


def reduce_end(upper, upper_got, lower, lower_got):
    return jnp.concatenate(
        [upper + upper_got.astype(F32), lower + lower_got.astype(F32)], axis=0
    )


def reduce_rows(here, away):
    return reduce_end(*reduce_second(*reduce_first(*reduce_start(here, away))))


def tie(*items):
    return lax.optimization_barrier(items)


def spread_y(block, y_at):
    rows, _, width = block.shape
    block = block.reshape(rows, 2, 2, width)
    return in_order(pick(block, y_at, 1), swap(pick(block, 1 - y_at, 1), "y"), y_at)


def spread_core(block, core_at):
    other = swap(pick(block, 1 - core_at, 2), "core")
    block = in_order(pick(block, core_at, 2), other, core_at)
    return jnp.swapaxes(block, 0, 1).reshape(-1, block.shape[-1])


def spread_others(block, y_at, core_at):
    rows, _, width = block.shape
    block = block.reshape(rows, 2, 2, width)
    near = pick(block, y_at, 1)
    far = swap(pick(block, 1 - y_at, 1), "y")
    got = swap(jnp.stack([pick(near, 1 - core_at, 1), pick(far, 1 - core_at, 1)]), "core")
    return jnp.stack([got[0], pick(far, core_at, 1), got[1]])


def in_place(own, others, quarter_at):
    size, rows, width = own.shape
    full = jnp.zeros((size, 4, rows, width), own.dtype)
    for other in range(4):
        block = own if other == 0 else others[:, other - 1]
        full = lax.dynamic_update_slice_in_dim(full, block[:, None], quarter_at ^ other, 1)
    return full.reshape(size * 4 * rows, width)


def gather_weights(block):
    return lax.all_gather(block, "z", axis=0, tiled=True)


def sum_weights(block):
    return lax.psum_scatter(block, "z", scatter_dimension=0, tiled=True)


def return_core(block, core_at):
    block = block.reshape(2, 2, -1, block.shape[1])
    return jnp.stack([pick(block, core_at, 1), swap(pick(block, 1 - core_at, 1), "core")])


def return_y(block, y_at):
    return pick(block, y_at, 1), swap(pick(block, 1 - y_at, 1), "y")


def return_weights(block, y_at, core_at):
    return return_y(return_core(block, core_at), y_at)


def sum_all(block, axes, size):
    step = 1
    while step < size:
        count = min(8, size // step)
        terms = [block] + [
            lax.ppermute(block, axes, [(i, i ^ (step * other)) for i in range(size)])
            for other in range(1, count)
        ]
        while len(terms) > 1:
            terms = [left + right for left, right in zip(terms[::2], terms[1::2])]
        block = terms[0]
        step *= count
    return block


def quarters(block):
    return block.reshape(block.shape[0], 4, -1)


def split_units(block, main):
    return quarters(block[:, : 4 * main]), quarters(block[:, 4 * main :])


def local(
    tokens,
    segment_ids,
    cotangent,
    w_qkv,
    m_qkv,
    v_qkv,
    w_out,
    m_out,
    v_out,
    w_gate_up,
    m_gate_up,
    v_gate_up,
    w_down,
    m_down,
    v_down,
    b_qkv,
    m_bias,
    v_bias,
    ln_params,
    m_norm,
    v_norm,
):
    share, model_width = tokens.shape
    length = segment_ids.shape[1]
    half_heads = b_qkv.shape[1]
    own_heads = half_heads // 4
    half_units = w_down.shape[0]
    main = half_units // 4 // LANES * LANES
    y_at = lax.axis_index("y")
    core_at = lax.axis_index("core")
    x_at = lax.axis_index("tensor")
    z_size = lax.axis_size("z")
    quarter_at = y_at * 2 + core_at

    w_qkv_low = w_qkv.astype(LOW)
    attn_block = jnp.concatenate(
        [quarters(w_qkv_low[k]) for k in range(3)] + [quarters(w_out.astype(LOW).T)], axis=2
    )
    gate_up_low = w_gate_up.astype(LOW)
    gate_main, gate_tail = split_units(gate_up_low[0], main)
    up_main, up_tail = split_units(gate_up_low[1], main)
    gate_up_block = jnp.concatenate([gate_main, up_main, gate_tail, up_tail], axis=2)
    down_main, down_tail = split_units(w_down.astype(LOW).T, main)
    down_block = jnp.concatenate([down_main, down_tail, jnp.zeros_like(down_tail)], axis=2)

    half = share // 2
    places = jnp.arange(half, dtype=jnp.int32)
    x_order = jnp.stack([x_at, 1 - x_at])
    positions = (
        jnp.arange(2, dtype=jnp.int32)[:, None, None] * half
        + x_order[None, :, None] * share
        + places[None, None, :]
    ).reshape(length)
    tables = angle_tables(positions)
    ids = segment_ids[0].reshape(2, 2, half)
    ids = jnp.swapaxes(jnp.where(x_at == 0, ids, ids[::-1]), 0, 1).reshape(length)
    bias = lax.dynamic_slice_in_dim(b_qkv, quarter_at * own_heads, own_heads, 1).reshape(1, -1)

    inputs_f = tokens.astype(F32)
    hat_a, scale_a = norm_stats(inputs_f)
    a_low = (hat_a * ln_params[0] + ln_params[1]).astype(LOW)
    attn_own = lax.all_gather(pick(attn_block, quarter_at, 1), "z")
    attn_block = spread_others(attn_block, y_at, core_at)
    attn_own, attn_block, a_low, ids, gate_up_block = tie(
        attn_own, attn_block, a_low, ids, gate_up_block
    )
    attn_full = in_place(attn_own, lax.all_gather(attn_block, "z"), quarter_at)
    gate_up_block = spread_y(gate_up_block, y_at)
    ids = jnp.stack([ids, swap(ids, "y")])
    flow, ids, gate_up_block = tie(gather_start(a_low), ids, gate_up_block)
    gate_up_block = spread_core(gate_up_block, core_at)
    ids = jnp.stack([ids, swap(ids, "core")]).reshape(4, length)
    row_info = jnp.stack([jnp.broadcast_to(positions, ids.shape), ids], axis=1)
    column_info = jnp.swapaxes(row_info, 1, 2)
    a_here, a_away = gather_end(*flow)
    a_here, gate_up_block, row_info, column_info, cot_low, down_block = tie(
        a_here, gate_up_block, row_info, column_info, cotangent, down_block
    )
    gate_up_full = gather_weights(gate_up_block)
    flow, down_block, a_here, a_away, attn_full = tie(
        gather_start(cot_low), spread_y(down_block, y_at), a_here, a_away, attn_full
    )
    down_block = spread_core(down_block, core_at)
    cot_here = gather_near(*flow)
    seq_info = (tables, row_info, column_info)
    a_rows_away, kept_away, mix_away, branch_away = attend(
        a_away, attn_full, bias, *seq_info, 2, LOW
    )
    down_full = gather_weights(down_block)
    a_rows_here, kept_here, mix_here, branch_here = attend(
        a_here, attn_full, bias, *seq_info, 0, F32
    )
    flow, cot_here = tie(reduce_start(branch_here, branch_away), cot_here)
    cot_away = tuple(swap(piece, "core") for piece in cot_here)
    flow = reduce_first(*flow)
    flow, cot_here, cot_away = tie(flow, collect(cot_here, length), collect(cot_away, length))
    middle = inputs_f + reduce_end(*reduce_second(*flow))
    hat_c, scale_c = norm_stats(middle)
    c_here, c_away = gather_rows((hat_c * ln_params[2] + ln_params[3]).astype(LOW))
    c_rows_here, gate_up_here, hidden_here = mlp(c_here, gate_up_full, length)
    c_rows_away, gate_up_away, hidden_away = mlp(c_away, gate_up_full, length)
    grad_down = grads(((cot_here, cot_away), (hidden_here, hidden_away)))
    cot_here, cot_away, grad_down = tie(cot_here, cot_away, grad_down)
    down_sum = sum_weights(grad_down)
    mlp_away, normed_away = mlp_back(cot_away, down_full, gate_up_away, length, gate_up_full)
    (mlp_here,) = mlp_back(cot_here, down_full, gate_up_here, length)
    flow = add_rows(mlp_here, gate_up_full, swap(normed_away, "core"), length)
    flow, mlp_here, mlp_away = tie(flow, mlp_here, mlp_away)
    grad_gate_up = grads(((c_rows_here, c_rows_away), (mlp_here, mlp_away)))
    flow, grad_gate_up, hidden_here, hidden_away = tie(
        reduce_first(*flow), grad_gate_up, hidden_here, hidden_away
    )
    gate_up_sum = sum_weights(grad_gate_up)
    result_away = dot(hidden_away, down_full, 1, 1).astype(LOW)
    flow, result_away, hidden_here = tie(reduce_second(*flow), result_away, hidden_here)
    d_normed_c = reduce_end(*flow)

    d_middle_n, d_gain_c, d_shift_c = norm_back(hat_c, scale_c, ln_params[2], d_normed_c)
    d_middle = cotangent.astype(F32) + d_middle_n
    result = add_rows(hidden_here, down_full, swap(result_away, "core"), length)
    flow, result = tie(gather_start(d_middle.astype(LOW)), result)
    branch_here, branch_away = gather_end(*flow)
    branch_here, result = tie(branch_here, result)
    result = reduce_first(*result)
    b_rows_here, back_here, normed_here = attend_back(
        branch_here, attn_full, kept_here, *seq_info, 0, F32
    )
    b_rows_away, back_away, normed_away = attend_back(
        branch_away, attn_full, kept_away, *seq_info, 2, LOW
    )
    down_sum = return_weights(down_sum, y_at, core_at)
    result, back_away, down_sum = tie(result, back_away, down_sum)
    grad_attn = grads(
        ((a_rows_here, a_rows_away), (back_here, back_away)),
        ((b_rows_here, b_rows_away), (mix_here, mix_away)),
    )
    grad_attn, normed_here, normed_away, back_here, back_away, result, down_sum = tie(
        grad_attn, normed_here, normed_away, back_here, back_away, result, down_sum
    )
    attn_sum = sum_weights(grad_attn)
    flow, gate_up_sum, down_sum = tie(
        reduce_first(*reduce_start(normed_here, normed_away)),
        return_core(gate_up_sum, core_at),
        down_sum,
    )
    flow, result, down_sum = tie(reduce_second(*flow), result, down_sum)
    d_normed_a = reduce_end(*flow)
    gate_up_sum = return_y(gate_up_sum, y_at)
    result = reduce_second(*result)
    d_input_n, d_gain_a, d_shift_a = norm_back(hat_a, scale_a, ln_params[0], d_normed_a)
    input_grad = d_middle + d_input_n

    bias_part = jnp.sum(back_here.astype(F32), axis=0) + jnp.sum(back_away.astype(F32), axis=0)
    bias_full = lax.dynamic_update_slice_in_dim(
        jnp.zeros((3, model_width), F32),
        bias_part.reshape(3, own_heads),
        x_at * half_heads + quarter_at * own_heads,
        1,
    )
    small = jnp.concatenate(
        [jnp.stack([d_gain_a, d_shift_a, d_gain_c, d_shift_c]), bias_full], axis=0
    )
    small = sum_all(small, "z", z_size)
    small, gate_up_sum, result = tie(small, gate_up_sum, result)
    small = sum_all(small, ("y", "core", "tensor"), 8)
    output = (middle + reduce_end(*result)).astype(LOW)
    norm_grad = small[:4]
    bias_grad = lax.dynamic_slice_in_dim(small[4:], x_at * half_heads, half_heads, 1)

    m_bias_new, v_bias_new, b_qkv_new = adamw_update(
        b_qkv, m_bias, v_bias, bias_grad, RATE_SMALL, 0.0
    )
    m_norm_new, v_norm_new, ln_params_new = adamw_update(
        ln_params, m_norm, v_norm, norm_grad, RATE_SMALL, 0.0
    )
    bias_new = (m_bias_new, v_bias_new, b_qkv_new)
    norm_new = (m_norm_new, v_norm_new, ln_params_new)
    attn_sum, output, input_grad, bias_new, norm_new, gate_up_sum, down_sum = tie(
        attn_sum, output, input_grad, bias_new, norm_new, gate_up_sum, down_sum
    )
    places = jnp.stack([y_at, core_at]).astype(jnp.int32)
    rows = w_qkv.shape[1]
    stacked = pl.BlockSpec((1, *w_gate_up.shape[1:]), lambda i, at: (i, 0, 0))
    gate_up_new = update(
        functools.partial(gate_up_update_kernel, main),
        2,
        [stacked] * 3,
        places,
        gate_up_sum,
        (w_gate_up, m_gate_up, v_gate_up),
    )
    flat = pl.BlockSpec(w_down.shape, lambda i, at: (0, 0))
    down_new = update(
        functools.partial(down_update_kernel, main),
        1,
        [flat] * 3,
        places,
        down_sum,
        (w_down, m_down, v_down),
    )
    qkv = pl.BlockSpec((3, rows, own_heads), lambda i, at: (0, 0, i))
    out = pl.BlockSpec((own_heads, rows), lambda i, at: (i, 0))
    attn_new = update(
        functools.partial(attn_update_kernel, own_heads),
        4,
        [qkv] * 3 + [out] * 3,
        places,
        return_weights(attn_sum, y_at, core_at),
        (w_qkv, m_qkv, v_qkv, w_out, m_out, v_out),
    )
    return (output, input_grad, *attn_new, *gate_up_new, *down_new, *bias_new, *norm_new)


def solution(mesh):
    owners = mesh.shape["dp"]
    pair = mesh.shape["tensor"]
    cut = Mesh(mesh.devices.reshape(owners // 4, 2, 2, pair), ("z", "y", "core", "tensor"))
    dp = ("z", "y", "core")
    rows = P((*dp, "tensor"), None)
    stacked = P(None, dp, "tensor")
    flat = P("tensor", dp)
    bias = P(None, "tensor")
    in_specs = (
        (rows, P(dp, None), rows)
        + (stacked,) * 3
        + (flat,) * 3
        + (stacked,) * 3
        + (flat,) * 3
        + (bias,) * 3
        + (P(),) * 3
    )
    out_specs = (
        (rows, rows)
        + (stacked,) * 3
        + (flat,) * 3
        + (stacked,) * 3
        + (flat,) * 3
        + (bias,) * 3
        + (P(),) * 3
    )
    return jax.shard_map(local, mesh=cut, in_specs=in_specs, out_specs=out_specs, check_vma=False)
```

```python
import functools

import jax
import jax.numpy as jnp
from jax import lax
from jax.experimental import pallas as pl
from jax.experimental.pallas import tpu as pltpu
from jax.sharding import Mesh
from jax.sharding import PartitionSpec as P

HD = 64
ROT = 16
STEP_COUNT = 10

EPS = 1e-05
NEG_FILL = -1000000000.0
BETA_ONE = 0.9
BETA_TWO = 0.95
ADAM_EPS = 1e-08
RATE_MATRIX = 0.01
RATE_OUT = 0.05
RATE_SMALL = 0.25
DECAY_MATRIX = 0.1

LOW = jnp.bfloat16
F32 = jnp.float32
LANES = 128
KERNEL_BYTES = 42 * 2**20


def dot(left, right, left_dim, right_dim):
    return lax.dot_general(
        left, right, (((left_dim,), (right_dim,)), ((), ())), preferred_element_type=F32
    )


def swap(block, axis):
    return lax.ppermute(block, axis, [(0, 1), (1, 0)])


def pick(block, index, dim):
    return lax.dynamic_index_in_dim(block, index, dim, keepdims=False)


def in_order(own, other, index):
    first = index == 0
    return jnp.stack([jnp.where(first, own, other), jnp.where(first, other, own)])


def norm_stats(row_data):
    average = jnp.mean(row_data, axis=-1, keepdims=True)
    centered = row_data - average
    variance = jnp.mean(centered * centered, axis=-1, keepdims=True)
    scale = lax.rsqrt(variance + EPS)
    return centered * scale, scale


def norm_back(hat, scale, gain_vec, grad):
    scaled = grad * gain_vec
    row_grad = (
        scaled
        - jnp.mean(scaled, axis=-1, keepdims=True)
        - hat * jnp.mean(scaled * hat, axis=-1, keepdims=True)
    ) * scale
    return row_grad, jnp.sum(grad * hat, axis=0), jnp.sum(grad, axis=0)


def angle_tables(positions):
    half_rot = ROT // 2
    frequency = 10000.0 ** (-2.0 * jnp.arange(half_rot, dtype=jnp.int32).astype(F32) / ROT)
    angle_table = positions.astype(F32)[:, None] * frequency[None, :]
    cos_part, sin_part = jnp.cos(angle_table), jnp.sin(angle_table)
    rest = jnp.zeros((positions.shape[0], HD - ROT), F32)
    none = jnp.zeros_like(sin_part)

    def table(*parts):
        return jnp.tile(jnp.concatenate(parts, axis=1), (1, LANES // HD))

    return (
        table(cos_part, cos_part, rest + 1.0),
        table(-sin_part, none, rest),
        table(none, sin_part, rest),
    )


def adamw_update(weight, first_mom, second, gradient, step_rate, decay_rate):
    first_mom = BETA_ONE * first_mom + (1.0 - BETA_ONE) * gradient
    second = BETA_TWO * second + (1.0 - BETA_TWO) * gradient * gradient
    fix_first = 1.0 - BETA_ONE**STEP_COUNT
    fix_second = 1.0 - BETA_TWO**STEP_COUNT
    update = first_mom / fix_first / (jnp.sqrt(second / fix_second) + ADAM_EPS)
    return (first_mom, second, weight - step_rate * (update + decay_rate * weight))


def turn(block, cos_t, low_t, high_t):
    return block * cos_t + pltpu.roll(block, LANES - ROT // 2, 1) * low_t + pltpu.roll(block, ROT // 2, 1) * high_t

def assemble(upper_ref, upper_far_ref, lower_ref, lower_far_ref, rows_ref):
    half = lower_ref.shape[1]

    @pl.when(pl.program_id(0) == 0)
    def near():
        rows_ref[: 2 * half] = upper_ref[...].reshape(2 * half, -1)

    @pl.when(pl.program_id(0) == 1)
    def far():
        rows_ref[: 2 * half] = upper_far_ref[...].reshape(2 * half, -1)

    rows_ref[2 * half : 3 * half] = lower_ref[0]
    rows_ref[3 * half :] = lower_far_ref[0]


def forward_kernel(
    own,
    upper_ref,
    upper_far_ref,
    lower_ref,
    lower_far_ref,
    weight_ref,
    bias_ref,
    cos_ref,
    low_ref,
    high_ref,
    row_ref,
    column_ref,
    rows_ref,
    keep_ref,
    mix_ref,
    branch_ref,
):
    assemble(upper_ref, upper_far_ref, lower_ref, lower_far_ref, rows_ref)
    rows = rows_ref[...]
    length = rows.shape[0]
    cos_t, low_t, high_t = cos_ref[...], low_ref[...], high_ref[...]
    allowed = (row_ref[0, 0:1] <= column_ref[0, :, 0:1]) & (
        row_ref[0, 1:2] == column_ref[0, :, 1:2]
    )
    first_head = lax.broadcasted_iota(jnp.int32, (length, LANES), 1) < HD
    scale = HD**-0.5
    for part in range(3):
        cols = slice(part * own, (part + 1) * own)
        made = dot(rows, weight_ref[:, cols], 1, 0) + bias_ref[:, cols]
        for at in range(0, own, LANES):
            piece = made[:, at : at + LANES]
            if part < 2:
                piece = turn(piece, cos_t, low_t, high_t)
            keep_ref[:, part * own + at : part * own + at + LANES] = piece.astype(LOW)
    for at in range(0, own, LANES):
        q2 = keep_ref[:, at : at + LANES]
        k2 = keep_ref[:, own + at : own + at + LANES]
        v2 = keep_ref[:, 2 * own + at : 2 * own + at + LANES]
        outs = []
        for head in range(2):
            mine = first_head if head == 0 else ~first_head
            scored = dot(jnp.where(mine, q2, jnp.zeros_like(q2)), k2, 1, 1) * scale
            scored = jnp.where(allowed, scored, NEG_FILL)
            exponent = jnp.exp(scored - jnp.max(scored, axis=1, keepdims=True))
            total = jnp.sum(exponent, axis=1, keepdims=True)
            outs.append(dot((exponent * (1.0 / total)).astype(LOW), v2, 1, 0))
        mix_ref[:, at : at + LANES] = jnp.where(first_head, outs[0], outs[1]).astype(LOW)
    branch_ref[...] = dot(mix_ref[...], weight_ref[:, 3 * own :], 1, 1).astype(branch_ref.dtype)


def backward_kernel(
    own,
    upper_ref,
    upper_far_ref,
    lower_ref,
    lower_far_ref,
    weight_ref,
    keep_ref,
    cos_ref,
    low_ref,
    high_ref,
    row_ref,
    column_ref,
    rows_ref,
    grad_ref,
    normed_ref,
):
    assemble(upper_ref, upper_far_ref, lower_ref, lower_far_ref, rows_ref)
    length = rows_ref.shape[0]
    cos_t, low_t, high_t = cos_ref[...], -low_ref[...], -high_ref[...]
    allowed = (column_ref[0, :, 0:1] <= row_ref[0, 0:1]) & (
        row_ref[0, 1:2] == column_ref[0, :, 1:2]
    )
    first_head = lax.broadcasted_iota(jnp.int32, (length, LANES), 1) < HD
    scale = HD**-0.5
    d_mix = dot(rows_ref[...], weight_ref[:, 3 * own :], 1, 0).astype(LOW)
    for at in range(0, own, LANES):
        q2 = keep_ref[:, at : at + LANES]
        k2 = keep_ref[:, own + at : own + at + LANES]
        v2 = keep_ref[:, 2 * own + at : 2 * own + at + LANES]
        do2 = d_mix[:, at : at + LANES]
        dq, dk, dv = [], [], []
        for head in range(2):
            mine = first_head if head == 0 else ~first_head
            scored = dot(jnp.where(mine, k2, jnp.zeros_like(k2)), q2, 1, 1) * scale
            scored = jnp.where(allowed, scored, NEG_FILL)
            exponent = jnp.exp(scored - jnp.max(scored, axis=0, keepdims=True))
            weights = exponent * (1.0 / jnp.sum(exponent, axis=0, keepdims=True))
            d_weights = dot(jnp.where(mine, v2, jnp.zeros_like(v2)), do2, 1, 1)
            total = jnp.sum(weights * d_weights, axis=0, keepdims=True)
            d_scores = (weights * (d_weights - total)).astype(LOW)
            dv.append(dot(weights.astype(LOW), do2, 1, 0))
            dk.append(dot(d_scores, q2, 1, 0))
            dq.append(dot(d_scores, k2, 0, 0))
        for part, pair in enumerate((dq, dk, dv)):
            piece = jnp.where(first_head, pair[0], pair[1])
            if part < 2:
                piece = turn(piece * scale, cos_t, low_t, high_t)
            grad_ref[:, part * own + at : part * own + at + LANES] = piece.astype(LOW)
    normed_ref[...] = dot(grad_ref[...], weight_ref[:, : 3 * own], 1, 1).astype(normed_ref.dtype)


def both_halves(block, first_half):
    other = pltpu.roll(block, LANES // 2, 1)
    return jnp.where(first_half, block, other), jnp.where(first_half, other, block)


def mlp_kernel(
    main,
    upper_ref,
    upper_far_ref,
    lower_ref,
    lower_far_ref,
    weight_ref,
    rows_ref,
    gate_up_ref,
    hidden_ref,
):
    assemble(upper_ref, upper_far_ref, lower_ref, lower_far_ref, rows_ref)
    rows = rows_ref[...]
    for at in range(0, 2 * main + LANES, 2 * LANES):
        cols = slice(at, min(at + 2 * LANES, 2 * main + LANES))
        gate_up_ref[:, cols] = dot(rows, weight_ref[:, cols], 1, 0)
    for at in range(0, main, LANES):
        gate = gate_up_ref[:, at : at + LANES]
        up = gate_up_ref[:, main + at : main + at + LANES]
        hidden_ref[:, at : at + LANES] = (gate / (1.0 + jnp.exp(-gate)) * up).astype(LOW)
    last = gate_up_ref[:, 2 * main :]
    first_half = lax.broadcasted_iota(jnp.int32, last.shape, 1) < LANES // 2
    gate, up = both_halves(last, first_half)
    made = gate / (1.0 + jnp.exp(-gate)) * up
    hidden_ref[:, main:] = jnp.where(first_half, made, 0.0).astype(LOW)


def gate_up_back(gate, up, d_hidden):
    sigma = 1.0 / (1.0 + jnp.exp(-gate))
    d_gate = d_hidden * up * sigma * (1.0 + gate * (1.0 - sigma))
    return d_gate.astype(LOW), (d_hidden * (gate * sigma)).astype(LOW)


def mlp_back_kernel(main, rows_ref, down_ref, gate_up_ref, grad_ref):
    rows = rows_ref[...]
    for start in range(0, main + LANES, 2 * LANES):
        d_hidden = dot(rows, down_ref[:, start : start + 2 * LANES], 1, 0)
        for at in range(start, min(start + 2 * LANES, main), LANES):
            d_gate, d_up = gate_up_back(
                gate_up_ref[:, at : at + LANES],
                gate_up_ref[:, main + at : main + at + LANES],
                d_hidden[:, at - start : at - start + LANES],
            )
            grad_ref[:, at : at + LANES] = d_gate
            grad_ref[:, main + at : main + at + LANES] = d_up
    last = gate_up_ref[:, 2 * main :]
    first_half = lax.broadcasted_iota(jnp.int32, last.shape, 1) < LANES // 2
    gate, up = both_halves(last, first_half)
    d_hidden, _ = both_halves(d_hidden[:, main - start :], first_half)
    d_gate, d_up = gate_up_back(gate, up, d_hidden)
    grad_ref[:, 2 * main :] = jnp.where(first_half, d_gate, d_up)


def mlp_back_send_kernel(main, rows_ref, down_ref, weight_ref, gate_up_ref, grad_ref, sent_ref):
    mlp_back_kernel(main, rows_ref, down_ref, gate_up_ref, grad_ref)
    sent_ref[...] = dot(grad_ref[...], weight_ref[...], 1, 1).astype(LOW)


def add_kernel(
    left_ref, right_ref, got_ref, upper_sent_ref, lower_sent_ref, upper_ref, lower_ref
):
    total = dot(left_ref[...], right_ref[...], 1, 1) + got_ref[...].astype(F32)
    half = lower_ref.shape[1]

    @pl.when(pl.program_id(0) == 0)
    def near():
        upper_ref[...] = total[: 2 * half].reshape(2, half, -1)

    @pl.when(pl.program_id(0) == 1)
    def far():
        upper_sent_ref[...] = total[: 2 * half].reshape(2, half, -1).astype(LOW)

    lower_ref[0] = total[2 * half : 3 * half]
    lower_sent_ref[0] = total[3 * half :].astype(LOW)


def whole(shape):
    return pl.BlockSpec(shape, lambda i: (0,) * len(shape))


HELD = pl.BlockSpec(memory_space=pltpu.VMEM)


def sequences(length, width, first=0):
    return pl.BlockSpec((length, width), lambda i: (first + i, 0))


def piece_specs(pieces):
    upper, _, lower, _ = pieces
    moving = pl.BlockSpec((1, *lower.shape[1:]), lambda i: (i, 0, 0))
    return [whole(upper.shape), whole(upper.shape), moving, moving]


def info_specs(length, first):
    return [
        pl.BlockSpec((1, 2, length), lambda i: (first + i, 0, 0)),
        pl.BlockSpec((1, length, 2), lambda i: (first + i, 0, 0)),
    ]


def call(kernel, in_specs, out_specs, out_shape, flops, operands):
    return pl.pallas_call(
        kernel,
        grid=(2,),
        in_specs=in_specs,
        out_specs=out_specs,
        out_shape=[jax.ShapeDtypeStruct(*item) for item in out_shape],
        compiler_params=pltpu.CompilerParams(vmem_limit_bytes=KERNEL_BYTES),
        cost_estimate=pl.CostEstimate(flops=flops, bytes_accessed=0, transcendentals=0),
    )(*operands)


def collect(pieces, length):
    width = pieces[0].shape[2]
    return call(
        assemble,
        piece_specs(pieces),
        [sequences(length, width)],
        [((2 * length, width), LOW)],
        0,
        pieces,
    )[0]


def attend(pieces, weight, bias, tables, row_info, column_info, first, kind):
    length = row_info.shape[2]
    count = 2 * length
    width = weight.shape[0]
    own = weight.shape[1] // 4
    return call(
        functools.partial(forward_kernel, own),
        piece_specs(pieces)
        + [whole(weight.shape), whole(bias.shape)]
        + [whole(table.shape) for table in tables]
        + info_specs(length, first),
        [sequences(length, item) for item in (width, 3 * own, own, width)],
        [
            ((count, width), LOW),
            ((count, 3 * own), LOW),
            ((count, own), LOW),
            ((count, width), kind),
        ],
        2 * count * (width * 4 * own + 4 * length * own),
        (*pieces, weight, bias, *tables, row_info, column_info),
    )


def attend_back(pieces, weight, kept, tables, row_info, column_info, first, kind):
    length = row_info.shape[2]
    count = 2 * length
    width = weight.shape[0]
    own = weight.shape[1] // 4
    return call(
        functools.partial(backward_kernel, own),
        piece_specs(pieces)
        + [whole(weight.shape), sequences(length, 3 * own)]
        + [whole(table.shape) for table in tables]
        + info_specs(length, first),
        [sequences(length, item) for item in (width, 3 * own, width)],
        [((count, width), LOW), ((count, 3 * own), LOW), ((count, width), kind)],
        2 * count * (width * 4 * own + 10 * length * own),
        (*pieces, weight, kept, *tables, row_info, column_info),
    )


def mlp(pieces, weight, length):
    count = 2 * length
    width, both = weight.shape
    main = (both - LANES) // 2
    return call(
        functools.partial(mlp_kernel, main),
        piece_specs(pieces) + [whole(weight.shape)],
        [sequences(length, item) for item in (width, both, main + LANES)],
        [((count, width), LOW), ((count, both), F32), ((count, main + LANES), LOW)],
        2 * count * width * both,
        (*pieces, weight),
    )


def mlp_back(rows, down, gate_up, length, weight=None):
    count = 2 * length
    width = rows.shape[1]
    both = gate_up.shape[1]
    specs = [sequences(length, width), HELD, sequences(length, both)]
    operands = [rows, down, gate_up]
    kernel, widths = mlp_back_kernel, (both,)
    if weight is not None:
        specs.insert(2, HELD)
        operands.insert(2, weight)
        kernel, widths = mlp_back_send_kernel, (both, width)
    return call(
        functools.partial(kernel, (both - LANES) // 2),
        specs,
        [sequences(length, item) for item in widths],
        [((count, item), LOW) for item in widths],
        (2 * len(widths) - 1) * count * width * both,
        operands,
    )


def add_rows(left, right, got, length):
    half = length // 4
    width = right.shape[0]
    shape = (2, half, width)
    moving = pl.BlockSpec((1, half, width), lambda i: (i, 0, 0))
    return call(
        add_kernel,
        [sequences(length, left.shape[1]), HELD, sequences(length, width)],
        [whole(shape), moving, whole(shape), moving],
        [(shape, LOW), (shape, LOW), (shape, F32), (shape, F32)],
        4 * length * width * left.shape[1],
        (left, right, got),
    )


def grads_kernel(widths, *refs):
    out_ref = refs[-1]
    at = 0
    for k, width in enumerate(widths):
        left_here, left_away, right_here, right_away = refs[4 * k : 4 * k + 4]
        made = dot(left_here[...], right_here[...], 0, 0) + dot(
            left_away[...], right_away[...], 0, 0
        )
        out_ref[:, at : at + width] = made.astype(LOW)
        at += width


def grads(*parts):
    operands, specs, widths, flops = [], [], [], 0
    for lefts, rights in parts:
        count, width = rights[0].shape
        depth = lefts[0].shape[1]
        block = min(512, depth)
        for half, left in enumerate(lefts):
            row = half if left.shape[0] == 2 * count else 0
            specs.append(pl.BlockSpec((count, block), lambda i, row=row: (row, i)))
        specs += [whole(right.shape) for right in rights]
        operands += [*lefts, *rights]
        widths.append(width)
        flops += 4 * count * depth * width
    total = sum(widths)
    return pl.pallas_call(
        functools.partial(grads_kernel, tuple(widths)),
        grid=(depth // block,),
        in_specs=specs,
        out_specs=pl.BlockSpec((block, total), lambda i: (i, 0)),
        out_shape=jax.ShapeDtypeStruct((depth, total), LOW),
        compiler_params=pltpu.CompilerParams(vmem_limit_bytes=KERNEL_BYTES),
        cost_estimate=pl.CostEstimate(flops=flops, bytes_accessed=0, transcendentals=0),
    )(*operands)


def adamw_write(refs, index, gradient, step_rate, decay_rate):
    weight, first_mom, second, new_first, new_second, new_weight = refs
    made = adamw_update(
        weight[index], first_mom[index], second[index], gradient, step_rate, decay_rate
    )
    new_first[index], new_second[index], new_weight[index] = made


def piece_of(at_ref, near_ref, far_ref, quarter, cols):
    y_away = lax.rem(quarter // 2 + at_ref[0], 2)
    core_away = lax.rem(lax.rem(quarter, 2) + at_ref[1], 2)
    near = near_ref[core_away, :, cols]
    return jnp.where(y_away == 0, near, far_ref[core_away, :, cols]).astype(F32)


def attn_update_kernel(own, at_ref, near_ref, far_ref, *refs):
    quarter = pl.program_id(0)
    qkv, out = refs[0:3] + refs[6:9], refs[3:6] + refs[9:12]
    for part in range(3):
        cols = slice(part * own, (part + 1) * own)
        gradient = piece_of(at_ref, near_ref, far_ref, quarter, cols)
        adamw_write(qkv, part, gradient, RATE_MATRIX, DECAY_MATRIX)
    gradient = piece_of(at_ref, near_ref, far_ref, quarter, slice(3 * own, 4 * own))
    adamw_write(out, slice(None), gradient.T, RATE_OUT, DECAY_MATRIX)


def gate_up_update_kernel(main, at_ref, near_ref, far_ref, *refs):
    part = pl.program_id(0)
    rows = near_ref.shape[1]
    first_half = lax.broadcasted_iota(jnp.int32, (rows, LANES), 1) < LANES // 2
    tails = []
    for quarter in range(4):
        cols = pl.ds(pl.multiple_of(part * main, LANES), main)
        gradient = piece_of(at_ref, near_ref, far_ref, quarter, cols)
        index = (0, slice(None), slice(quarter * main, (quarter + 1) * main))
        adamw_write(refs, index, gradient, RATE_MATRIX, DECAY_MATRIX)
        last = piece_of(at_ref, near_ref, far_ref, quarter, slice(2 * main, 2 * main + LANES))
        tails.append((last, pltpu.roll(last, LANES // 2, 1)))
    for pair in range(2):
        (left, left_turned), (right, right_turned) = tails[2 * pair : 2 * pair + 2]
        left = jnp.where(part == 0, left, left_turned)
        right = jnp.where(part == 0, right_turned, right)
        at = 4 * main + pair * LANES
        index = (0, slice(None), slice(at, at + LANES))
        adamw_write(
            refs, index, jnp.where(first_half, left, right), RATE_MATRIX, DECAY_MATRIX
        )


def down_update_kernel(main, at_ref, near_ref, far_ref, *refs):
    for quarter in range(4):
        gradient = piece_of(at_ref, near_ref, far_ref, quarter, slice(0, main + LANES)).T
        for source, at, size in (
            (0, quarter * main, main),
            (main, 4 * main + quarter * (LANES // 2), LANES // 2),
        ):
            adamw_write(
                refs,
                slice(at, at + size),
                gradient[source : source + size],
                RATE_MATRIX,
                DECAY_MATRIX,
            )


def update(kernel, steps, specs, places, pieces, arrays):
    near, far = pieces
    return pl.pallas_call(
        kernel,
        grid_spec=pltpu.PrefetchScalarGridSpec(
            num_scalar_prefetch=1,
            grid=(steps,),
            in_specs=[pl.BlockSpec(near.shape, lambda i, at: (0, 0, 0))] * 2 + specs,
            out_specs=specs,
        ),
        out_shape=[jax.ShapeDtypeStruct(array.shape, F32) for array in arrays],
        compiler_params=pltpu.CompilerParams(vmem_limit_bytes=KERNEL_BYTES),
        cost_estimate=pl.CostEstimate(
            flops=0, bytes_accessed=24 * sum(array.size for array in arrays) // 3, transcendentals=0
        ),
    )(places, near, far, *arrays)


def gather_start(rows):
    half = rows.shape[0] // 2
    upper, lower = rows[:half], rows[half:]
    return upper, swap(upper, "tensor"), lower, swap(lower, "y")


def gather_near(upper, upper_x, lower, lower_y):
    upper_pair = jnp.stack([upper, upper_x])
    lower_pair = jnp.stack([lower, lower_y])
    return upper_pair, swap(upper_pair, "y"), lower_pair, swap(lower_pair, "tensor")


def gather_end(*flow):
    here = gather_near(*flow)
    return here, tuple(swap(piece, "core") for piece in here)


def gather_rows(rows):
    return gather_end(*gather_start(rows))


def reduce_start(here, away):
    away = swap(away, "core")
    total = (here.astype(F32) + away.astype(F32)).reshape(2, 2, 2, -1, here.shape[1])
    upper, lower = total[:, 0], total[:, 1]
    return upper[1].astype(LOW), lower[:, 1].astype(LOW), upper[0], lower[:, 0]


def reduce_first(upper_sent, lower_sent, upper, lower):
    return upper, swap(upper_sent, "y"), lower, swap(lower_sent, "tensor")


def reduce_second(upper, upper_got, lower, lower_got):
    upper = upper + upper_got.astype(F32)
    lower = lower + lower_got.astype(F32)
    return (
        upper[0],
        swap(upper[1].astype(LOW), "tensor"),
        lower[0],
        swap(lower[1].astype(LOW), "y"),
    )


def reduce_end(upper, upper_got, lower, lower_got):
    return jnp.concatenate(
        [upper + upper_got.astype(F32), lower + lower_got.astype(F32)], axis=0
    )


def reduce_rows(here, away):
    return reduce_end(*reduce_second(*reduce_first(*reduce_start(here, away))))


def tie(*items):
    return lax.optimization_barrier(items)


def spread_y(block, y_at):
    rows, _, width = block.shape
    block = block.reshape(rows, 2, 2, width)
    return in_order(pick(block, y_at, 1), swap(pick(block, 1 - y_at, 1), "y"), y_at)


def spread_core(block, core_at):
    other = swap(pick(block, 1 - core_at, 2), "core")
    block = in_order(pick(block, core_at, 2), other, core_at)
    return jnp.swapaxes(block, 0, 1).reshape(-1, block.shape[-1])


def pack_kernel(own, at_ref, qkv_ref, out_ref, own_ref, rest_ref):
    def pack(packed_ref):
        for part in range(3):
            packed_ref[0, :, part * own : (part + 1) * own] = qkv_ref[part].astype(LOW)
        packed_ref[0, :, 3 * own :] = out_ref[...].T.astype(LOW)

    @pl.when(pl.program_id(0) == 0)
    def first():
        pack(own_ref)

    @pl.when(pl.program_id(0) > 0)
    def others():
        pack(rest_ref)


def pack_attn(w_qkv, w_out, own, place):
    rows = w_qkv.shape[1]
    block = (1, rows, 4 * own)
    return pl.pallas_call(
        functools.partial(pack_kernel, own),
        grid_spec=pltpu.PrefetchScalarGridSpec(
            num_scalar_prefetch=1,
            grid=(4,),
            in_specs=[
                pl.BlockSpec((3, rows, own), lambda i, at: (0, 0, at[0] ^ i)),
                pl.BlockSpec((own, rows), lambda i, at: (at[0] ^ i, 0)),
            ],
            out_specs=[
                pl.BlockSpec(block, lambda i, at: (0, 0, 0)),
                pl.BlockSpec(block, lambda i, at: (jnp.maximum(i - 1, 0), 0, 0)),
            ],
        ),
        out_shape=[jax.ShapeDtypeStruct((size, *block[1:]), LOW) for size in (1, 3)],
        compiler_params=pltpu.CompilerParams(vmem_limit_bytes=56 * 2**20),
        cost_estimate=pl.CostEstimate(flops=0, bytes_accessed=0, transcendentals=0),
    )(place, w_qkv, w_out)


def spread_others(rest):
    far = swap(rest[1:], "y")
    got = swap(jnp.stack([rest[0], far[1]]), "core")
    return jnp.stack([got[0], far[0], got[1]])


def in_place(own, others, quarter_at):
    size, rows, width = own.shape
    full = jnp.zeros((size, 4, rows, width), own.dtype)
    for other in range(4):
        block = own if other == 0 else others[:, other - 1]
        full = lax.dynamic_update_slice_in_dim(full, block[:, None], quarter_at ^ other, 1)
    return full.reshape(size * 4 * rows, width)


def gather_weights(block):
    return lax.all_gather(block, "z", axis=0, tiled=True)


def sum_weights(block):
    return lax.psum_scatter(block, "z", scatter_dimension=0, tiled=True)


def return_core(block, core_at):
    block = block.reshape(2, 2, -1, block.shape[1])
    return jnp.stack([pick(block, core_at, 1), swap(pick(block, 1 - core_at, 1), "core")])


def return_y(block, y_at):
    return pick(block, y_at, 1), swap(pick(block, 1 - y_at, 1), "y")


def return_weights(block, y_at, core_at):
    return return_y(return_core(block, core_at), y_at)


def sum_all(block, axes, size):
    step = 1
    while step < size:
        count = min(8, size // step)
        terms = [block] + [
            lax.ppermute(block, axes, [(i, i ^ (step * other)) for i in range(size)])
            for other in range(1, count)
        ]
        while len(terms) > 1:
            terms = [left + right for left, right in zip(terms[::2], terms[1::2])]
        block = terms[0]
        step *= count
    return block


def quarters(block):
    return block.reshape(block.shape[0], 4, -1)


def split_units(block, main):
    return quarters(block[:, : 4 * main]), quarters(block[:, 4 * main :])


def local(
    tokens,
    segment_ids,
    cotangent,
    w_qkv,
    m_qkv,
    v_qkv,
    w_out,
    m_out,
    v_out,
    w_gate_up,
    m_gate_up,
    v_gate_up,
    w_down,
    m_down,
    v_down,
    b_qkv,
    m_bias,
    v_bias,
    ln_params,
    m_norm,
    v_norm,
):
    share, model_width = tokens.shape
    length = segment_ids.shape[1]
    half_heads = b_qkv.shape[1]
    own_heads = half_heads // 4
    half_units = w_down.shape[0]
    main = half_units // 4 // LANES * LANES
    y_at = lax.axis_index("y")
    core_at = lax.axis_index("core")
    x_at = lax.axis_index("tensor")
    z_size = lax.axis_size("z")
    quarter_at = y_at * 2 + core_at

    place = quarter_at.astype(jnp.int32).reshape(1)
    attn_own, attn_block = pack_attn(w_qkv, w_out, own_heads, place)
    gate_up_low = w_gate_up.astype(LOW)
    gate_main, gate_tail = split_units(gate_up_low[0], main)
    up_main, up_tail = split_units(gate_up_low[1], main)
    gate_up_block = jnp.concatenate([gate_main, up_main, gate_tail, up_tail], axis=2)
    down_main, down_tail = split_units(w_down.astype(LOW).T, main)
    down_block = jnp.concatenate([down_main, down_tail, jnp.zeros_like(down_tail)], axis=2)

    half = share // 2
    places = jnp.arange(half, dtype=jnp.int32)
    x_order = jnp.stack([x_at, 1 - x_at])
    positions = (
        jnp.arange(2, dtype=jnp.int32)[:, None, None] * half
        + x_order[None, :, None] * share
        + places[None, None, :]
    ).reshape(length)
    tables = angle_tables(positions)
    ids = segment_ids[0].reshape(2, 2, half)
    ids = jnp.swapaxes(jnp.where(x_at == 0, ids, ids[::-1]), 0, 1).reshape(length)
    bias = lax.dynamic_slice_in_dim(b_qkv, quarter_at * own_heads, own_heads, 1).reshape(1, -1)

    inputs_f = tokens.astype(F32)
    hat_a, scale_a = norm_stats(inputs_f)
    a_low = (hat_a * ln_params[0] + ln_params[1]).astype(LOW)
    attn_own = lax.all_gather(attn_own[0], "z")
    attn_block = spread_others(attn_block)
    attn_own, attn_block, a_low, ids, gate_up_block = tie(
        attn_own, attn_block, a_low, ids, gate_up_block
    )
    attn_full = in_place(attn_own, lax.all_gather(attn_block, "z"), quarter_at)
    gate_up_block = spread_y(gate_up_block, y_at)
    ids = jnp.stack([ids, swap(ids, "y")])
    flow, ids, gate_up_block = tie(gather_start(a_low), ids, gate_up_block)
    gate_up_block = spread_core(gate_up_block, core_at)
    ids = jnp.stack([ids, swap(ids, "core")]).reshape(4, length)
    row_info = jnp.stack([jnp.broadcast_to(positions, ids.shape), ids], axis=1)
    column_info = jnp.swapaxes(row_info, 1, 2)
    a_here, a_away = gather_end(*flow)
    a_here, gate_up_block, row_info, column_info, cot_low, down_block = tie(
        a_here, gate_up_block, row_info, column_info, cotangent, down_block
    )
    gate_up_full = gather_weights(gate_up_block)
    flow, down_block, a_here, a_away, attn_full = tie(
        gather_start(cot_low), spread_y(down_block, y_at), a_here, a_away, attn_full
    )
    down_block = spread_core(down_block, core_at)
    cot_here = gather_near(*flow)
    seq_info = (tables, row_info, column_info)
    a_rows_away, kept_away, mix_away, branch_away = attend(
        a_away, attn_full, bias, *seq_info, 2, LOW
    )
    down_full = gather_weights(down_block)
    a_rows_here, kept_here, mix_here, branch_here = attend(
        a_here, attn_full, bias, *seq_info, 0, F32
    )
    flow, cot_here = tie(reduce_start(branch_here, branch_away), cot_here)
    cot_away = tuple(swap(piece, "core") for piece in cot_here)
    flow = reduce_first(*flow)
    flow, cot_here, cot_away = tie(flow, collect(cot_here, length), collect(cot_away, length))
    middle = inputs_f + reduce_end(*reduce_second(*flow))
    hat_c, scale_c = norm_stats(middle)
    c_here, c_away = gather_rows((hat_c * ln_params[2] + ln_params[3]).astype(LOW))
    c_rows_here, gate_up_here, hidden_here = mlp(c_here, gate_up_full, length)
    c_rows_away, gate_up_away, hidden_away = mlp(c_away, gate_up_full, length)
    grad_down = grads(((cot_here, cot_away), (hidden_here, hidden_away)))
    cot_here, cot_away, grad_down = tie(cot_here, cot_away, grad_down)
    down_sum = sum_weights(grad_down)
    mlp_away, normed_away = mlp_back(cot_away, down_full, gate_up_away, length, gate_up_full)
    (mlp_here,) = mlp_back(cot_here, down_full, gate_up_here, length)
    flow = add_rows(mlp_here, gate_up_full, swap(normed_away, "core"), length)
    flow, mlp_here, mlp_away = tie(flow, mlp_here, mlp_away)
    grad_gate_up = grads(((c_rows_here, c_rows_away), (mlp_here, mlp_away)))
    flow, grad_gate_up, hidden_here, hidden_away = tie(
        reduce_first(*flow), grad_gate_up, hidden_here, hidden_away
    )
    gate_up_sum = sum_weights(grad_gate_up)
    result_away = dot(hidden_away, down_full, 1, 1).astype(LOW)
    flow, result_away, hidden_here = tie(reduce_second(*flow), result_away, hidden_here)
    d_normed_c = reduce_end(*flow)

    d_middle_n, d_gain_c, d_shift_c = norm_back(hat_c, scale_c, ln_params[2], d_normed_c)
    d_middle = cotangent.astype(F32) + d_middle_n
    result = add_rows(hidden_here, down_full, swap(result_away, "core"), length)
    flow, result = tie(gather_start(d_middle.astype(LOW)), result)
    branch_here, branch_away = gather_end(*flow)
    branch_here, result = tie(branch_here, result)
    result = reduce_first(*result)
    b_rows_here, back_here, normed_here = attend_back(
        branch_here, attn_full, kept_here, *seq_info, 0, F32
    )
    b_rows_away, back_away, normed_away = attend_back(
        branch_away, attn_full, kept_away, *seq_info, 2, LOW
    )
    down_sum = return_weights(down_sum, y_at, core_at)
    result, back_away, down_sum = tie(result, back_away, down_sum)
    grad_attn = grads(
        ((a_rows_here, a_rows_away), (back_here, back_away)),
        ((b_rows_here, b_rows_away), (mix_here, mix_away)),
    )
    grad_attn, normed_here, normed_away, back_here, back_away, result, down_sum = tie(
        grad_attn, normed_here, normed_away, back_here, back_away, result, down_sum
    )
    attn_sum = sum_weights(grad_attn)
    flow, gate_up_sum, down_sum = tie(
        reduce_first(*reduce_start(normed_here, normed_away)),
        return_core(gate_up_sum, core_at),
        down_sum,
    )
    flow, result, down_sum = tie(reduce_second(*flow), result, down_sum)
    d_normed_a = reduce_end(*flow)
    gate_up_sum = return_y(gate_up_sum, y_at)
    result = reduce_second(*result)
    d_input_n, d_gain_a, d_shift_a = norm_back(hat_a, scale_a, ln_params[0], d_normed_a)
    input_grad = d_middle + d_input_n

    bias_part = jnp.sum(back_here.astype(F32), axis=0) + jnp.sum(back_away.astype(F32), axis=0)
    bias_full = lax.dynamic_update_slice_in_dim(
        jnp.zeros((3, model_width), F32),
        bias_part.reshape(3, own_heads),
        x_at * half_heads + quarter_at * own_heads,
        1,
    )
    small = jnp.concatenate(
        [jnp.stack([d_gain_a, d_shift_a, d_gain_c, d_shift_c]), bias_full], axis=0
    )
    small = sum_all(small, "z", z_size)
    small, gate_up_sum, result = tie(small, gate_up_sum, result)
    small = sum_all(small, ("y", "core", "tensor"), 8)
    output = (middle + reduce_end(*result)).astype(LOW)
    norm_grad = small[:4]
    bias_grad = lax.dynamic_slice_in_dim(small[4:], x_at * half_heads, half_heads, 1)

    m_bias_new, v_bias_new, b_qkv_new = adamw_update(
        b_qkv, m_bias, v_bias, bias_grad, RATE_SMALL, 0.0
    )
    m_norm_new, v_norm_new, ln_params_new = adamw_update(
        ln_params, m_norm, v_norm, norm_grad, RATE_SMALL, 0.0
    )
    bias_new = (m_bias_new, v_bias_new, b_qkv_new)
    norm_new = (m_norm_new, v_norm_new, ln_params_new)
    attn_sum, output, input_grad, bias_new, norm_new, gate_up_sum, down_sum = tie(
        attn_sum, output, input_grad, bias_new, norm_new, gate_up_sum, down_sum
    )
    places = jnp.stack([y_at, core_at]).astype(jnp.int32)
    rows = w_qkv.shape[1]
    stacked = pl.BlockSpec((1, *w_gate_up.shape[1:]), lambda i, at: (i, 0, 0))
    gate_up_new = update(
        functools.partial(gate_up_update_kernel, main),
        2,
        [stacked] * 3,
        places,
        gate_up_sum,
        (w_gate_up, m_gate_up, v_gate_up),
    )
    flat = pl.BlockSpec(w_down.shape, lambda i, at: (0, 0))
    down_new = update(
        functools.partial(down_update_kernel, main),
        1,
        [flat] * 3,
        places,
        down_sum,
        (w_down, m_down, v_down),
    )
    qkv = pl.BlockSpec((3, rows, own_heads), lambda i, at: (0, 0, i))
    out = pl.BlockSpec((own_heads, rows), lambda i, at: (i, 0))
    attn_new = update(
        functools.partial(attn_update_kernel, own_heads),
        4,
        [qkv] * 3 + [out] * 3,
        places,
        return_weights(attn_sum, y_at, core_at),
        (w_qkv, m_qkv, v_qkv, w_out, m_out, v_out),
    )
    return (output, input_grad, *attn_new, *gate_up_new, *down_new, *bias_new, *norm_new)


def solution(mesh):
    owners = mesh.shape["dp"]
    pair = mesh.shape["tensor"]
    cut = Mesh(mesh.devices.reshape(owners // 4, 2, 2, pair), ("z", "y", "core", "tensor"))
    dp = ("z", "y", "core")
    rows = P((*dp, "tensor"), None)
    stacked = P(None, dp, "tensor")
    flat = P("tensor", dp)
    bias = P(None, "tensor")
    in_specs = (
        (rows, P(dp, None), rows)
        + (stacked,) * 3
        + (flat,) * 3
        + (stacked,) * 3
        + (flat,) * 3
        + (bias,) * 3
        + (P(),) * 3
    )
    out_specs = (
        (rows, rows)
        + (stacked,) * 3
        + (flat,) * 3
        + (stacked,) * 3
        + (flat,) * 3
        + (bias,) * 3
        + (P(),) * 3
    )
    return jax.shard_map(local, mesh=cut, in_specs=in_specs, out_specs=out_specs, check_vma=False)
```
